1024 devices in a mesh: expert: 64 (over z, x), dp: 16 (over y, core).
Axes of the slice: x: 4, y: 8, z: 16, core: 2. Of those that a mesh axis runs over, the one named last changes fastest.
Arguments:
- cotangent: bfloat16 [16, 12288, 1024], P('dp', 'expert'), may hold values from -4 to 4
- route_weights: float32 [16, 12288, 8], P('dp', 'expert'), may hold values from 0.02 to 0.5
- expert_ids: int32 [16, 12288, 8], P('dp', 'expert'), may hold values from 0 to 63, as said below
- slot_index: int32 [16, 12288, 8], P('dp', 'expert'), may hold values from 0 to 23, as said below
- hidden: bfloat16 [16, 64, 1536, 384], P('dp', 'expert'), may hold values from -6 to 6
- carried_error: bfloat16 [16, 64, 384, 1024], P('dp', 'expert'), may hold values from -6 to 6
- q_factor: float32 [64, 16, 1024], P('expert'), may hold values from -0.1875 to 0.1875
Outputs:
- new_error: bfloat16 [16, 64, 384, 1024], P('dp', 'expert')
- q_next: float32 [64, 16, 1024], P('expert')
The draws below stay inside these ranges and needn't reach their ends.
Inputs may be any that keep to these rules, and one draw needn't show every extreme that they name: `expert_ids`: each token names 8 different experts. The tokens of one device name one expert at most 24 times, and in each replica one expert is named exactly 24 times by the tokens of every device of that replica. `slot_index`: among the tokens of one device, the routes to one expert carry different slots.
All inputs are finite; a program needn't handle non-finite values.
Results may differ from the reference program's by a relative error of at most 0.017.
Values may be sent and summed in bfloat16 or wider, within the bound.
A program may use at most 32 MiB of HBM per device.

```python
import math
import jax
import jax.numpy as jnp
from jax import lax

D = 1024
FF = 384
TOP = 8
RANK = 16
TOK_DEV = 192
EXPERTS = 64
TOK_REP = 12288
SEND = 24
CAP = 1536
N_EXPERT = 64
N_DP = 16


def slot_shuffle(slot_key):
    return jax.random.permutation(slot_key, SEND)


def device_routes(device_key, hot_expert):
    key_offsets, key_order, key_tokens, key_rotation, key_slots = jax.random.split(device_key, 5)
    offsets = jax.random.permutation(key_offsets, EXPERTS)[:TOP].astype(jnp.int32)
    targets = (hot_expert - offsets) % EXPERTS
    labels = jnp.arange(EXPERTS, dtype=jnp.int32)
    member = jnp.any(labels[:, None] == targets[None, :], axis=1)
    scores = jax.random.permutation(key_order, EXPERTS).astype(jnp.int32) + jnp.where(member, 0, EXPERTS)
    ordering = jnp.argsort(scores).astype(jnp.int32)
    starts = ordering[jnp.arange(TOK_DEV, dtype=jnp.int32) % EXPERTS]
    starts = starts[jax.random.permutation(key_tokens, TOK_DEV)]
    rotation = jax.random.randint(key_rotation, (TOK_DEV,), 0, TOP)
    column = (jnp.arange(TOP, dtype=jnp.int32)[None, :] + rotation[:, None]) % TOP
    chosen = (starts[:, None] + offsets[column]) % EXPERTS
    flattened = chosen.reshape(-1)
    onehot = (flattened[:, None] == labels[None, :]).astype(jnp.int32)
    ranking = jnp.sum((jnp.cumsum(onehot, axis=0) - 1) * onehot, axis=1)
    shuffles = jax.vmap(slot_shuffle)(jax.random.split(key_slots, EXPERTS)).astype(jnp.int32)
    slot_values = shuffles[flattened, ranking].reshape(TOK_DEV, TOP)
    return (chosen.astype(jnp.int32), slot_values.astype(jnp.int32))


def routing(key):
    key_hot, key_devices = jax.random.split(key)
    hot_expert = jax.random.randint(key_hot, (N_DP,), 0, EXPERTS)
    numbers = jnp.arange(N_DP * N_EXPERT, dtype=jnp.int32)
    device_keys = jax.vmap(partial_fold(key_devices))(numbers)
    hot_each = hot_expert[numbers // N_EXPERT]
    chosen, slot_values = jax.vmap(device_routes)(device_keys, hot_each)
    return (chosen.reshape(N_DP, N_EXPERT * TOK_DEV, TOP), slot_values.reshape(N_DP, N_EXPERT * TOK_DEV, TOP))


def partial_fold(base_key):

    def folded(number):
        return jax.random.fold_in(base_key, number)
    return folded


def draw_expert_ids(key, part):
    shared = routing(key)
    return shared[0]


def draw_slot_index(key, part):
    shared = routing(key)
    return shared[1]


def steps_of(stream_key, shape, pieces, low, high):
    def one(dim, shards_of):
        heights = jax.random.uniform(jax.random.fold_in(jax.random.fold_in(stream_key, 6), dim), (shards_of,), jnp.float32, low / len(pieces), high / len(pieces))
        return jnp.repeat(jnp.exp(heights), shape[dim] // shards_of).reshape((-1,) + (1,) * (len(shape) - dim - 1))

    gain = one(*pieces[0])
    for cut in pieces[1:]:
        gain = gain * one(*cut)
    return gain


def scatter_about(stream_key, extent, deviation, reach, shards=(), kind=jnp.bfloat16):
    result = jax.random.normal(stream_key, extent, jnp.float32) * deviation
    if len(shards) > 0:
        result = steps_of(stream_key, extent, shards, -0.22, 0.18) * result
    return jnp.clip(result, min=-reach, max=reach).astype(kind)


def setup_inputs(seed: int = 0) -> dict:
    seeds = jax.random.split(jax.random.key(seed), 8)
    return {
        "cotangent": scatter_about(seeds[0], (N_DP, TOK_REP, D), 0.25, 4.0, ((0, 16), (1, 64))),
        "route_weights": jnp.clip(jnp.exp(math.log(0.5) - 3.218876 * jax.random.uniform(seeds[1], (N_DP, TOK_REP, TOP), jnp.float32) ** steps_of(seeds[1], (N_DP, TOK_REP, TOP), ((0, 16), (1, 64)), -0.2, 0.2)), 0.02, 0.5),
        "expert_ids": draw_expert_ids(jax.random.fold_in(seeds[7], 71), 0),
        "slot_index": draw_slot_index(jax.random.fold_in(seeds[7], 71), 0),
        "hidden": scatter_about(seeds[4], (N_DP, EXPERTS, CAP, FF), 1.0, 6.0, ((0, 16), (1, 64))),
        "carried_error": scatter_about(seeds[5], (N_DP, EXPERTS, FF, D), 0.5, 6.0, ((0, 16), (1, 64))),
        "q_factor": scatter_about(seeds[6], (EXPERTS, RANK, D), D ** -0.5, 0.1875, ((0, 64),), jnp.float32),
    }


highest = lax.Precision.HIGHEST

def orthonormal(factor_rows):
    gram_matrix = jnp.dot(factor_rows, factor_rows.T, precision=highest)
    lower_factor = jnp.linalg.cholesky(gram_matrix)
    return lax.linalg.triangular_solve(lower_factor, factor_rows, left_side=True, lower=True)

def expert_product(operands):
    return jnp.dot(operands[0].astype(jnp.float32).T, operands[1].astype(jnp.float32), precision=highest)

def replica_merged(operands):
    cotangent, route_weights, expert_ids, slot_index, hidden, carried_error = operands
    scaled = (route_weights[:, :, None] * cotangent[:, None, :].astype(jnp.float32)).astype(jnp.bfloat16)
    source = (jnp.arange(TOK_REP) // TOK_DEV).astype(jnp.int32)
    target = (expert_ids.astype(jnp.int32) * CAP + source[:, None] * SEND + slot_index.astype(jnp.int32)).reshape(-1)
    placed = jnp.zeros((EXPERTS * CAP, D), jnp.bfloat16).at[target].set(scaled.reshape(-1, D))
    placed = placed.reshape(EXPERTS, CAP, D)
    gradient = lax.map(expert_product, (hidden, placed))
    return gradient + carried_error.astype(jnp.float32)

def reference(cotangent, route_weights, expert_ids, slot_index, hidden, carried_error, q_factor):
    merged = lax.map(replica_merged, (cotangent, route_weights, expert_ids, slot_index, hidden, carried_error))
    left_sum = jnp.einsum('erd,nefd->erf', q_factor, merged, precision=highest) / N_DP
    basis_rows = jax.vmap(orthonormal)(left_sum)
    q_next = jnp.einsum('erf,nefd->erd', basis_rows, merged, precision=highest) / N_DP
    approx = jnp.einsum('erf,erd->efd', basis_rows, q_next, precision=highest)
    new_error = (merged - approx[None]).astype(jnp.bfloat16)
    return (new_error, q_next)
```

```python
import functools

import jax
import jax.numpy as jnp
from jax import lax
from jax.experimental import pallas as pl
from jax.experimental.pallas import tpu as pltpu
from jax.sharding import PartitionSpec as P

highest = lax.Precision.HIGHEST
MESH = pl.DeviceIdType.MESH
f32 = jnp.float32
bf16 = jnp.bfloat16

X_CHIPS = 4
PARTS = 4
PAD = 32


def thirds(value):
    first = value.astype(bf16).astype(f32)
    second = (value - first).astype(bf16).astype(f32)
    return first, second, value - first - second


def route_kernel(
    nz, nx, send,
    cot, weights, ids, slots, hidden_hbm, error_hbm, merged,
    ring, meta, own_meta, picked, arrived, picked_own, arrived_own, picked_far, arrived_far,
    hidden, error,
    local_sem, ring_send, ring_recv, meta_send, meta_recv, x_send, x_recv,
):
    half = nz // 2
    tokens, model_dim = cot.shape
    width = model_dim // PARTS
    lanes = nx * send
    me = lax.axis_index("expert")
    z = lax.div(me, nx)
    x = lax.rem(me, nx)
    right = lax.rem(z + 1, nz) * nx + x
    left = lax.rem(z + nz - 1, nz) * nx + x
    sides = (right, left)

    load_hidden = pltpu.make_async_copy(hidden_hbm, hidden, local_sem.at[0])
    load_error = pltpu.make_async_copy(error_hbm, error, local_sem.at[1])
    load_hidden.start()
    load_error.start()

    barrier = pltpu.get_barrier_semaphore()
    partners = [right, left] + [z * nx + lax.rem(x + step, nx) for step in range(1, nx)]
    for partner in partners:
        pl.semaphore_signal(barrier, inc=1, device_id={"expert": partner}, device_id_type=MESH)
    pl.semaphore_wait(barrier, len(partners))

    def ring_copy(side, hop, part, source=None):
        return pltpu.make_async_remote_copy(
            src_ref=ring.at[side, hop - 2, part] if source is None else source,
            dst_ref=ring.at[side, hop - 1, part],
            send_sem=ring_send.at[side, hop - 1, part],
            recv_sem=ring_recv.at[side, hop - 1, part],
            device_id={"expert": sides[side]},
            device_id_type=MESH,
        )

    def own_copy(side, part):
        return ring_copy(side, 1, part, cot.at[:, pl.ds(part * width, width)])

    def meta_copy(side, hop):
        return pltpu.make_async_remote_copy(
            src_ref=meta.at[side, hop - 1],
            dst_ref=meta.at[side, hop],
            send_sem=meta_send.at[side, hop - 1],
            recv_sem=meta_recv.at[side, hop - 1],
            device_id={"expert": sides[side]},
            device_id_type=MESH,
        )

    def x_copy(pick, land, group, part, step, source=None):
        target = lax.rem(x + step, nx)
        source = x if source is None else source
        return pltpu.make_async_remote_copy(
            src_ref=pick.at[part, target],
            dst_ref=land.at[part, source],
            send_sem=x_send.at[group, part, step - 1],
            recv_sem=x_recv.at[group, part, step - 1],
            device_id={"expert": z * nx + target},
            device_id_type=MESH,
        )

    for part in range(PARTS):
        for side in range(2):
            own_copy(side, part).start()

    lane = lax.broadcasted_iota(jnp.int32, (tokens, 128), 1)
    token = lax.broadcasted_iota(jnp.int32, (tokens, 128), 0).astype(f32)
    level = lax.div(ids[...], nx)
    place = lax.rem(ids[...], nx) * send + slots[...]
    to_right = lax.rem(level - z - 1 + 2 * nz, nz)
    to_left = lax.rem(z - level - 1 + 2 * nz, nz)
    table = jnp.zeros((128, 512), f32)
    for k in range(ids.shape[1]):
        row = (lane == to_right[:, k : k + 1]) | (lane == 16 + to_left[:, k : k + 1])
        hit = lane == place[:, k : k + 1]
        values = [token] + list(thirds(jnp.broadcast_to(weights[:, k : k + 1], (tokens, 128))))
        values = jnp.concatenate([jnp.where(hit, v, 0.0) for v in values], axis=1).astype(bf16)
        table += lax.dot_general(
            jnp.where(row, 1.0, 0.0).astype(bf16), values, (((0,), (0,)), ((), ())),
            preferred_element_type=f32,
        )
    which = table[:, :128]
    gain = (table[:, 384:] + table[:, 256:384]) + table[:, 128:256]
    for side in range(2):
        meta[side, 0, 0:8, :] = which[16 * side : 16 * side + 8]
        meta[side, 0, 8:16, :] = gain[16 * side : 16 * side + 8]
        meta_copy(side, 1).start()
    own_meta[0:16, :] = which[0:16]
    own_meta[16:32, :] = gain[0:16]

    token_lane = lax.broadcasted_iota(jnp.int32, (lanes, tokens), 1).astype(f32)

    def columns(rows):
        stacked = jnp.concatenate(rows + [jnp.zeros((8 - len(rows), 128), f32)], axis=0)
        turned = jnp.transpose(stacked)[:lanes]
        return [turned[:, i : i + 1] for i in range(len(rows))]

    def one_hot(which_column):
        return jnp.where(token_lane == which_column, 1.0, 0.0).astype(bf16)

    def pick_rows(blocks, pick, land, group, part, rows):
        chosen = [
            jnp.dot(choice, block, preferred_element_type=f32) * scale
            for choice, scale, block in blocks
        ]
        pad = rows - send * len(blocks)
        filler = [jnp.zeros((pad, width), f32)] if pad else []
        for target in range(nx):
            cut = [c[target * send : (target + 1) * send] for c in chosen]
            pick[part, target] = jnp.concatenate(cut + filler, axis=0).astype(bf16)
        for step in range(1, nx):
            x_copy(pick, land, group, part, step).start()
        land[part, x] = pick[part, x]

    def hidden_rows(levels, rows):
        blocks = [hidden[v].astype(f32) for v in levels]
        pad = rows - send * len(levels)
        filler = [jnp.zeros((pad, hidden.shape[2]), f32)] if pad else []
        pieces = []
        for source in range(nx):
            pieces += [b[source * send : (source + 1) * send] for b in blocks] + filler
        return jnp.transpose(jnp.concatenate(pieces, axis=0)).astype(bf16)

    def accumulate(land, pick, group, levels, rows, order=range(PARTS)):
        turned = hidden_rows(levels, rows)
        for part in order:
            for step in range(1, nx):
                x_copy(pick, land, group, part, step, lax.rem(x + nx - step, nx)).wait_recv()
            block = land[part].reshape(nx * rows, width)
            merged[:, pl.ds(part * width, width)] += jnp.dot(
                turned, block, preferred_element_type=f32
            )

    def pair_levels(hop):
        return [lax.rem(z - hop + nz, nz), lax.rem(z + hop, nz)]

    def step_hop(hop, forward):
        choices = None
        for part in range(PARTS):
            for side in range(2):
                ring_copy(side, hop, part, cot.at[:, pl.ds(0, width)]).wait_recv()
                if forward(side, part):
                    ring_copy(side, hop + 1, part).start()
            if choices is None:
                for side in range(2):
                    meta_copy(side, hop).wait_recv()
                    if forward(side, None):
                        meta_copy(side, hop + 1).start()
                got = columns(
                    [meta[s, hop, pl.ds(hop - 1, 1), :] for s in range(2)]
                    + [meta[s, hop, pl.ds(hop + 7, 1), :] for s in range(2)]
                )
                choices = [(one_hot(got[s]), got[2 + s]) for s in range(2)]
            blocks = [choices[s] + (ring[s, hop - 1, part],) for s in range(2)]
            pick_rows(blocks, picked.at[hop - 1], arrived.at[hop - 1], hop - 1, part, 2 * send)

    def add_hop(hop):
        accumulate(arrived.at[hop - 1], picked.at[hop - 1], hop - 1, pair_levels(hop), 2 * send)

    got = columns([own_meta[nz - 1 : nz, :], own_meta[nz + 15 : nz + 16, :]])
    own_choice = (one_hot(got[0]), got[1])
    for part in range(PARTS):
        block = cot[:, part * width : (part + 1) * width]
        pick_rows([own_choice + (block,)], picked_own, arrived_own, half - 1, part, PAD)
    load_error.wait()
    merged[...] = error[...].astype(f32)
    load_hidden.wait()

    everything = lambda side, part: True
    last = lambda side, part: (side == 0) if part is None else (part < PARTS // 2) == (side == 0)
    step_hop(1, everything)
    accumulate(arrived_own, picked_own, half - 1, [z], PAD)

    def body(hop, carry):
        step_hop(hop, everything)
        add_hop(hop - 1)
        return carry

    lax.fori_loop(2, half - 1, body, 0)
    step_hop(half - 1, last)
    add_hop(half - 2)

    meta_copy(0, half).wait_recv()
    got = columns([meta[0, half, half - 1 : half, :], meta[0, half, half + 7 : half + 8, :]])
    far_choice = (one_hot(got[0]), got[1])
    order = []
    for part in range(PARTS // 2):
        order += [(0, part), (1, part + PARTS // 2)]
    for side, part in order:
        ring_copy(side, half, part, cot.at[:, pl.ds(0, width)]).wait_recv()
        block = ring[side, half - 1, part]
        pick_rows([far_choice + (block,)], picked_far, arrived_far, half, part, PAD)
    add_hop(half - 1)
    far = lax.rem(z + half, nz)
    accumulate(arrived_far, picked_far, half, [far], PAD, [part for _, part in order])

    for part in range(PARTS):
        for side in range(2):
            own_copy(side, part).wait_send()
    for side in range(2):
        meta_copy(side, 1).wait_send()

    def drain(hop, carry):
        for part in range(PARTS):
            for side in range(2):
                ring_copy(side, hop, part).wait_send()
        for side in range(2):
            meta_copy(side, hop).wait_send()
        return carry

    lax.fori_loop(2, half, drain, 0)
    for side, part in order:
        ring_copy(side, half, part).wait_send()
    meta_copy(0, half).wait_send()

    def drain_x(group, carry):
        for part in range(PARTS):
            for step in range(1, nx):
                x_copy(picked.at[group], arrived.at[group], group, part, step).wait_send()
        return carry

    lax.fori_loop(0, half - 1, drain_x, 0)
    for pick, land, group in (
        (picked_own, arrived_own, half - 1),
        (picked_far, arrived_far, half),
    ):
        for part in range(PARTS):
            for step in range(1, nx):
                x_copy(pick, land, group, part, step).wait_send()


def factor_kernel(
    replicas,
    merged, q_rows, new_error, q_next,
    left_out, left_in, left_all, right_out, right_in, right_all, send_sem, recv_sem,
):
    me = lax.axis_index("dp")
    rank = q_rows.shape[0]

    if replicas > 1:
        barrier = pltpu.get_barrier_semaphore()
        for step in range(1, replicas):
            pl.semaphore_signal(
                barrier, inc=1, device_id={"dp": lax.rem(me + step, replicas)}, device_id_type=MESH
            )
        pl.semaphore_wait(barrier, replicas - 1)

    share = rank // replicas

    def copy(source, target, stage, step, origin):
        return pltpu.make_async_remote_copy(
            src_ref=source,
            dst_ref=target.at[origin],
            send_sem=send_sem.at[stage, step - 1],
            recv_sem=recv_sem.at[stage, step - 1],
            device_id={"dp": lax.rem(me + step, replicas)},
            device_id_type=MESH,
        )

    def begin_sum(value, out, into, stage):
        for row in range(rank):
            out[row // share, row % share] = value[row : row + 1]
        for step in range(1, replicas):
            copy(out.at[lax.rem(me + step, replicas)], into, stage, step, me).start()
        into[me] = out[me]

    def end_sum(out, into, gathered, stage):
        for step in range(1, replicas):
            origin = lax.rem(me + replicas - step, replicas)
            copy(out.at[0], into, stage, step, origin).wait_recv()
        total = into[0]
        for origin in range(1, replicas):
            total += into[origin]
        gathered[me] = total * (1.0 / replicas)
        for step in range(1, replicas):
            copy(gathered.at[me], gathered, stage + 1, step, me).start()

    def collect(gathered, stage):
        for step in range(1, replicas):
            origin = lax.rem(me + replicas - step, replicas)
            copy(gathered.at[me], gathered, stage + 1, step, origin).wait_recv()
        return jnp.concatenate(
            [gathered[row // share, row % share] for row in range(rank)], axis=0
        )

    left_local = lax.dot_general(
        q_rows[...], merged[...], (((1,), (1,)), ((), ())),
        precision=highest, preferred_element_type=f32,
    )
    begin_sum(left_local, left_out, left_in, 0)
    end_sum(left_out, left_in, left_all, 0)
    left_sum = collect(left_all, 0)

    right_local = jnp.dot(left_sum, merged[...], precision=highest, preferred_element_type=f32)
    begin_sum(right_local, right_out, right_in, 2)

    gram = lax.dot_general(
        left_sum, left_sum, (((1,), (1,)), ((), ())),
        precision=highest, preferred_element_type=f32,
    )
    rows = lax.broadcasted_iota(jnp.int32, (rank, rank), 0)
    cols = lax.broadcasted_iota(jnp.int32, (rank, rank), 1)
    unit = jnp.where(rows == cols, 1.0, 0.0)
    row_of = lax.broadcasted_iota(jnp.int32, (rank, 1), 0)
    inverse = unit
    pivots = jnp.zeros((rank, 1), f32)
    for k in range(rank):
        pivot = gram[k : k + 1, k : k + 1]
        pivots = jnp.where(row_of == k, pivot, pivots)
        ratio = jnp.where(row_of > k, gram[:, k : k + 1] / pivot, 0.0)
        gram, inverse = gram - ratio * gram[k : k + 1], inverse - ratio * inverse[k : k + 1]
    inverse = inverse / jnp.sqrt(pivots)
    basis = jnp.dot(inverse, left_sum, precision=highest, preferred_element_type=f32)

    end_sum(right_out, right_in, right_all, 2)
    right_sum = collect(right_all, 2)
    q_new = jnp.dot(inverse, right_sum, precision=highest, preferred_element_type=f32)
    q_next[...] = q_new
    approx = lax.dot_general(
        basis, q_new, (((0,), (0,)), ((), ())), precision=highest, preferred_element_type=f32
    )
    new_error[...] = (merged[...] - approx).astype(bf16)

    for stage, source in enumerate((left_out, left_all, right_out, right_all)):
        for step in range(1, replicas):
            copy(source.at[0], source, stage, step, me).wait_send()


def shards(cotangent, route_weights, expert_ids, slot_index, hidden, carried_error, q_factor):
    peers = lax.axis_size("expert")
    replicas = lax.axis_size("dp")
    nx = X_CHIPS
    nz = peers // nx
    half = nz // 2
    tokens, model_dim = cotangent.shape[1:]
    capacity, ff = hidden.shape[2:]
    send = capacity // peers
    width = model_dim // PARTS
    vmem = pl.BlockSpec(memory_space=pltpu.VMEM)
    anywhere = pl.BlockSpec(memory_space=pl.ANY)
    dma = pltpu.SemaphoreType.DMA
    merged = pl.pallas_call(
        functools.partial(route_kernel, nz, nx, send),
        out_shape=jax.ShapeDtypeStruct((ff, model_dim), f32),
        in_specs=[vmem] * 4 + [anywhere] * 2,
        out_specs=vmem,
        scratch_shapes=[
            pltpu.VMEM((2, half, PARTS, tokens, width), bf16),
            pltpu.VMEM((2, half + 1, 16, 128), f32),
            pltpu.VMEM((32, 128), f32),
            pltpu.VMEM((half - 1, PARTS, nx, 2 * send, width), bf16),
            pltpu.VMEM((half - 1, PARTS, nx, 2 * send, width), bf16),
        ]
        + [pltpu.VMEM((PARTS, nx, PAD, width), bf16)] * 4
        + [
            pltpu.VMEM((nz, nx * send, ff), bf16),
            pltpu.VMEM((ff, model_dim), bf16),
            dma((2,)),
            dma((2, half, PARTS)),
            dma((2, half, PARTS)),
            dma((2, half)),
            dma((2, half)),
            dma((half + 1, PARTS, nx - 1)),
            dma((half + 1, PARTS, nx - 1)),
        ],
        compiler_params=pltpu.CompilerParams(
            collective_id=0, has_side_effects=True, vmem_limit_bytes=48 * 1024 * 1024
        ),
        name="route",
    )(
        cotangent[0],
        route_weights[0],
        expert_ids[0],
        slot_index[0],
        hidden[0, 0].reshape(nz, nx * send, ff),
        carried_error[0, 0],
    )
    rank = q_factor.shape[1]
    share = rank // replicas
    new_error, q_next = pl.pallas_call(
        functools.partial(factor_kernel, replicas),
        out_shape=(
            jax.ShapeDtypeStruct((ff, model_dim), bf16),
            jax.ShapeDtypeStruct((rank, model_dim), f32),
        ),
        in_specs=[vmem] * 2,
        out_specs=(vmem, vmem),
        scratch_shapes=[pltpu.VMEM((replicas, share, 1, ff), f32)] * 3
        + [pltpu.VMEM((replicas, share, 1, model_dim), f32)] * 3
        + [dma((4, replicas - 1 if replicas > 1 else 1))] * 2,
        compiler_params=pltpu.CompilerParams(
            collective_id=1, has_side_effects=True, vmem_limit_bytes=48 * 1024 * 1024
        ),
        name="factor",
    )(merged, q_factor[0])
    return (new_error[None, None], q_next[None])


def solution(mesh):
    return jax.shard_map(
        shards,
        mesh=mesh,
        in_specs=(
            P("dp", "expert", None),
            P("dp", "expert", None),
            P("dp", "expert", None),
            P("dp", "expert", None),
            P("dp", "expert", None, None),
            P("dp", "expert", None, None),
            P("expert", None, None),
        ),
        out_specs=(P("dp", "expert", None, None), P("expert", None, None)),
        check_vma=False,
    )
```

```python
import functools

import jax
import jax.numpy as jnp
from jax import lax
from jax.experimental import pallas as pl
from jax.experimental.pallas import tpu as pltpu
from jax.sharding import PartitionSpec as P

highest = lax.Precision.HIGHEST
MESH = pl.DeviceIdType.MESH
f32 = jnp.float32
bf16 = jnp.bfloat16

X_CHIPS = 4
PARTS = 4
VMEM_BYTES = 60 * 1024 * 1024
PAD = 32


def thirds(value):
    first = value.astype(bf16).astype(f32)
    second = (value - first).astype(bf16).astype(f32)
    return first, second, value - first - second


def kernel(
    nz, nx, send, replicas,
    cot, weights, ids, slots, hidden_hbm, error_hbm, q_rows, new_error, q_next,
    merged, splits, own, ring, meta, own_meta, picked, arrived, picked_own, arrived_own, picked_far, arrived_far,
    hidden, error,
    left_out, left_in, left_all, right_out, right_in, right_all,
    local_sem, ring_send, ring_recv, meta_send, meta_recv, x_send, x_recv, dp_send, dp_recv,
):
    half = nz // 2
    tokens, model_dim = cot.shape
    width = model_dim // PARTS
    lanes = nx * send
    me = lax.axis_index("expert")
    z = lax.div(me, nx)
    x = lax.rem(me, nx)
    right = lax.rem(z + 1, nz) * nx + x
    left = lax.rem(z + nz - 1, nz) * nx + x
    sides = (right, left)

    load_hidden = pltpu.make_async_copy(hidden_hbm, hidden, local_sem.at[0])
    load_error = pltpu.make_async_copy(error_hbm, error, local_sem.at[1])
    load_own = pltpu.make_async_copy(cot, own, local_sem.at[2])
    load_own.start()
    load_hidden.start()
    load_error.start()

    barrier = pltpu.get_barrier_semaphore()
    partners = [right, left] + [z * nx + lax.rem(x + step, nx) for step in range(1, nx)]
    for partner in partners:
        pl.semaphore_signal(barrier, inc=1, device_id={"expert": partner}, device_id_type=MESH)
    replica = lax.axis_index("dp")
    for step in range(1, replicas):
        partner = lax.rem(replica + step, replicas)
        pl.semaphore_signal(barrier, inc=1, device_id={"dp": partner}, device_id_type=MESH)
    pl.semaphore_wait(barrier, len(partners) + replicas - 1)

    def ring_copy(side, hop, part, source=None):
        return pltpu.make_async_remote_copy(
            src_ref=ring.at[side, hop - 2, part] if source is None else source,
            dst_ref=ring.at[side, hop - 1, part],
            send_sem=ring_send.at[side, hop - 1, part],
            recv_sem=ring_recv.at[side, hop - 1, part],
            device_id={"expert": sides[side]},
            device_id_type=MESH,
        )

    def own_copy(side, part):
        return ring_copy(side, 1, part, cot.at[:, pl.ds(part * width, width)])

    def meta_copy(side, hop):
        return pltpu.make_async_remote_copy(
            src_ref=meta.at[side, hop - 1],
            dst_ref=meta.at[side, hop],
            send_sem=meta_send.at[side, hop - 1],
            recv_sem=meta_recv.at[side, hop - 1],
            device_id={"expert": sides[side]},
            device_id_type=MESH,
        )

    def x_copy(pick, land, group, part, step, source=None):
        target = lax.rem(x + step, nx)
        source = x if source is None else source
        return pltpu.make_async_remote_copy(
            src_ref=pick.at[part, target],
            dst_ref=land.at[part, source],
            send_sem=x_send.at[group, part, step - 1],
            recv_sem=x_recv.at[group, part, step - 1],
            device_id={"expert": z * nx + target},
            device_id_type=MESH,
        )

    for part in range(PARTS):
        for side in range(2):
            own_copy(side, part).start()

    routes = ids.shape[0]
    spot = lax.broadcasted_iota(jnp.int32, (128, tokens), 0)
    token = lax.broadcasted_iota(jnp.int32, (128, tokens), 1).astype(f32)
    level = lax.div(ids[...], nx)
    place = lax.rem(ids[...], nx) * send + slots[...]
    to_right = lax.rem(level - z - 1 + 2 * nz, nz)
    to_left = lax.rem(z - level - 1 + 2 * nz, nz) + 16
    table = jnp.zeros((32, 512), f32)
    for k in range(routes):
        row = (spot[:32] == to_right[k : k + 1]) | (spot[:32] == to_left[k : k + 1])
        hit = spot == place[k : k + 1]
        values = [token] + [
            jnp.broadcast_to(v, (128, tokens)) for v in thirds(weights[k : k + 1, :])
        ]
        values = jnp.concatenate([jnp.where(hit, v, 0.0) for v in values], axis=0).astype(bf16)
        table += lax.dot_general(
            jnp.where(row, 1.0, 0.0).astype(bf16), values, (((1,), (1,)), ((), ())),
            preferred_element_type=f32,
        )
    which = table[:, :128]
    gain = (table[:, 384:] + table[:, 256:384]) + table[:, 128:256]
    for side in range(2):
        meta[side, 0, 0:8, :] = which[16 * side : 16 * side + 8]
        meta[side, 0, 8:16, :] = gain[16 * side : 16 * side + 8]
        meta_copy(side, 1).start()
    own_meta[0:16, :] = which[0:16]
    own_meta[16:32, :] = gain[0:16]

    token_lane = lax.broadcasted_iota(jnp.int32, (lanes, tokens), 1).astype(f32)

    def columns(rows):
        stacked = jnp.concatenate(rows + [jnp.zeros((8 - len(rows), 128), f32)], axis=0)
        turned = jnp.transpose(stacked)[:lanes]
        return [turned[:, i : i + 1] for i in range(len(rows))]

    def one_hot(which_column):
        return jnp.where(token_lane == which_column, 1.0, 0.0).astype(bf16)

    def pick_rows(blocks, pick, land, group, part, rows):
        chosen = [
            jnp.dot(choice, block, preferred_element_type=f32) * scale
            for choice, scale, block in blocks
        ]
        pad = rows - send * len(blocks)
        filler = [jnp.zeros((pad, width), f32)] if pad else []
        for target in range(nx):
            cut = [c[target * send : (target + 1) * send] for c in chosen]
            pick[part, target] = jnp.concatenate(cut + filler, axis=0).astype(bf16)
        for step in range(1, nx):
            x_copy(pick, land, group, part, step).start()
        land[part, x] = pick[part, x]

    def hidden_rows(levels, rows):
        blocks = [hidden[v].astype(f32) for v in levels]
        pad = rows - send * len(levels)
        filler = [jnp.zeros((pad, hidden.shape[2]), f32)] if pad else []
        pieces = []
        for source in range(nx):
            pieces += [b[source * send : (source + 1) * send] for b in blocks] + filler
        return jnp.transpose(jnp.concatenate(pieces, axis=0)).astype(bf16)

    def accumulate(land, pick, group, levels, rows, order=range(PARTS), then=None):
        turned = hidden_rows(levels, rows)
        for part in order:
            for step in range(1, nx):
                x_copy(pick, land, group, part, step, lax.rem(x + nx - step, nx)).wait_recv()
            block = land[part].reshape(nx * rows, width)
            merged[:, pl.ds(part * width, width)] += jnp.dot(
                turned, block, preferred_element_type=f32
            )
            if then is not None:
                then(part)

    def pair_levels(hop):
        return [lax.rem(z - hop + nz, nz), lax.rem(z + hop, nz)]

    def step_hop(hop, forward):
        choices = None
        for part in range(PARTS):
            for side in range(2):
                ring_copy(side, hop, part, cot.at[:, pl.ds(0, width)]).wait_recv()
                if forward(side, part):
                    ring_copy(side, hop + 1, part).start()
            if choices is None:
                for side in range(2):
                    meta_copy(side, hop).wait_recv()
                    if forward(side, None):
                        meta_copy(side, hop + 1).start()
                got = columns(
                    [meta[s, hop, pl.ds(hop - 1, 1), :] for s in range(2)]
                    + [meta[s, hop, pl.ds(hop + 7, 1), :] for s in range(2)]
                )
                choices = [(one_hot(got[s]), got[2 + s]) for s in range(2)]
            blocks = [choices[s] + (ring[s, hop - 1, part],) for s in range(2)]
            pick_rows(blocks, picked.at[hop - 1], arrived.at[hop - 1], hop - 1, part, 2 * send)

    def add_hop(hop):
        accumulate(arrived.at[hop - 1], picked.at[hop - 1], hop - 1, pair_levels(hop), 2 * send)

    load_own.wait()
    got = columns([own_meta[nz - 1 : nz, :], own_meta[nz + 15 : nz + 16, :]])
    own_choice = (one_hot(got[0]), got[1])
    for part in range(PARTS):
        block = own[:, part * width : (part + 1) * width]
        pick_rows([own_choice + (block,)], picked_own, arrived_own, half - 1, part, PAD)
    load_error.wait()
    merged[...] = error[...].astype(f32)
    load_hidden.wait()

    everything = lambda side, part: True
    last = lambda side, part: (side == 0) if part is None else (part < PARTS // 2) == (side == 0)
    step_hop(1, everything)
    accumulate(arrived_own, picked_own, half - 1, [z], PAD)

    def body(hop, carry):
        step_hop(hop, everything)
        add_hop(hop - 1)
        return carry

    lax.fori_loop(2, half - 1, body, 0)
    step_hop(half - 1, last)
    add_hop(half - 2)

    meta_copy(0, half).wait_recv()
    got = columns([meta[0, half, half - 1 : half, :], meta[0, half, half + 7 : half + 8, :]])
    far_choice = (one_hot(got[0]), got[1])
    order = []
    for part in range(PARTS // 2):
        order += [(0, part), (1, part + PARTS // 2)]
    for side, part in order:
        ring_copy(side, half, part, cot.at[:, pl.ds(0, width)]).wait_recv()
        block = ring[side, half - 1, part]
        pick_rows([far_choice + (block,)], picked_far, arrived_far, half, part, PAD)
    add_hop(half - 1)
    far = lax.rem(z + half, nz)
    rank = q_rows.shape[0]
    ff = merged.shape[0]
    q_parts = thirds(q_rows[...])
    blank = jnp.zeros((128 - 3 * rank, model_dim), f32)
    none = jnp.zeros((rank, model_dim), f32)
    q_stacks = [
        jnp.concatenate(list(q_parts[: 3 - i]) + [none] * i + [blank], axis=0).astype(bf16)
        for i in range(3)
    ]
    left_turned = [jnp.zeros((ff, 128), f32)]

    def left_product(part):
        cols = slice(part * width, (part + 1) * width)
        for i, piece in enumerate(thirds(merged[:, cols])):
            piece = piece.astype(bf16)
            splits[i, :, cols] = piece
            left_turned[0] += lax.dot_general(
                piece, q_stacks[i][:, cols], (((1,), (1,)), ((), ())), preferred_element_type=f32
            )

    accumulate(
        arrived_far, picked_far, half, [far], PAD, [part for _, part in order], left_product
    )
    stacked = jnp.transpose(left_turned[0])
    left_local = (stacked[2 * rank : 3 * rank] + stacked[rank : 2 * rank]) + stacked[:rank]

    share = rank // replicas

    def dp_copy(source, target, stage, step, origin):
        return pltpu.make_async_remote_copy(
            src_ref=source,
            dst_ref=target.at[origin],
            send_sem=dp_send.at[stage, step - 1],
            recv_sem=dp_recv.at[stage, step - 1],
            device_id={"dp": lax.rem(replica + step, replicas)},
            device_id_type=MESH,
        )

    def begin_sum(value, out, into, stage):
        for row in range(rank):
            out[row // share, row % share] = value[row : row + 1]
        for step in range(1, replicas):
            target = lax.rem(replica + step, replicas)
            dp_copy(out.at[target], into, stage, step, replica).start()
        into[replica] = out[replica]

    def end_sum(out, into, gathered, stage):
        for step in range(1, replicas):
            origin = lax.rem(replica + replicas - step, replicas)
            dp_copy(out.at[0], into, stage, step, origin).wait_recv()
        total = into[0]
        for origin in range(1, replicas):
            total += into[origin]
        gathered[replica] = total * (1.0 / replicas)
        for step in range(1, replicas):
            dp_copy(gathered.at[replica], gathered, stage + 1, step, replica).start()

    def collect(gathered, stage):
        for step in range(1, replicas):
            origin = lax.rem(replica + replicas - step, replicas)
            dp_copy(gathered.at[replica], gathered, stage + 1, step, origin).wait_recv()
        return jnp.concatenate(
            [gathered[row // share, row % share] for row in range(rank)], axis=0
        )

    begin_sum(left_local, left_out, left_in, 0)

    for part in range(PARTS):
        for side in range(2):
            own_copy(side, part).wait_send()
    for side in range(2):
        meta_copy(side, 1).wait_send()

    def drain(hop, carry):
        for part in range(PARTS):
            for side in range(2):
                ring_copy(side, hop, part).wait_send()
        for side in range(2):
            meta_copy(side, hop).wait_send()
        return carry

    lax.fori_loop(2, half, drain, 0)
    for side, part in order:
        ring_copy(side, half, part).wait_send()
    meta_copy(0, half).wait_send()

    def drain_x(group, carry):
        for part in range(PARTS):
            for step in range(1, nx):
                x_copy(picked.at[group], arrived.at[group], group, part, step).wait_send()
        return carry

    lax.fori_loop(0, half - 1, drain_x, 0)
    for pick, land, group in (
        (picked_own, arrived_own, half - 1),
        (picked_far, arrived_far, half),
    ):
        for part in range(PARTS):
            for step in range(1, nx):
                x_copy(pick, land, group, part, step).wait_send()

    end_sum(left_out, left_in, left_all, 0)
    left_sum = collect(left_all, 0)

    left_parts = thirds(left_sum)
    left_stack = jnp.concatenate(left_parts, axis=0).astype(bf16)
    right_local = None
    for i in (2, 1, 0):
        product = jnp.dot(left_stack[: (3 - i) * rank], splits[i], preferred_element_type=f32)
        for j in range(2 - i, -1, -1):
            term = product[j * rank : (j + 1) * rank]
            right_local = term if right_local is None else right_local + term
    begin_sum(right_local, right_out, right_in, 2)

    gram = lax.dot_general(
        left_sum, left_sum, (((1,), (1,)), ((), ())),
        precision=highest, preferred_element_type=f32,
    )
    rows = lax.broadcasted_iota(jnp.int32, (rank, rank), 0)
    cols = lax.broadcasted_iota(jnp.int32, (rank, rank), 1)
    row_of = lax.broadcasted_iota(jnp.int32, (rank, 1), 0)
    inverse = jnp.where(rows == cols, 1.0, 0.0)
    pivots = jnp.zeros((rank, 1), f32)
    for k in range(rank):
        pivot = gram[k : k + 1, k : k + 1]
        pivots = jnp.where(row_of == k, pivot, pivots)
        ratio = jnp.where(row_of > k, gram[:, k : k + 1] / pivot, 0.0)
        gram, inverse = gram - ratio * gram[k : k + 1], inverse - ratio * inverse[k : k + 1]
    inverse = inverse / jnp.sqrt(pivots)
    basis = jnp.dot(inverse, left_sum, precision=highest, preferred_element_type=f32)
    b1, b2, b3 = thirds(basis)
    basis_stack = jnp.transpose(jnp.concatenate([b1, b1, b1, b2, b2, b3], axis=0)).astype(bf16)

    end_sum(right_out, right_in, right_all, 2)
    right_sum = collect(right_all, 2)
    q_new = jnp.dot(inverse, right_sum, precision=highest, preferred_element_type=f32)
    q_next[...] = q_new
    p1, p2, p3 = thirds(q_new)
    q_stack = jnp.concatenate([p1, p2, p3, p1, p2, p1], axis=0).astype(bf16)
    for part in range(PARTS):
        cols = slice(part * width, (part + 1) * width)
        approx = jnp.dot(basis_stack, q_stack[:, cols], preferred_element_type=f32)
        new_error[:, cols] = (merged[:, cols] - approx).astype(bf16)

    for stage, source in enumerate((left_out, left_all, right_out, right_all)):
        for step in range(1, replicas):
            dp_copy(source.at[0], source, stage, step, replica).wait_send()


def shards(cotangent, route_weights, expert_ids, slot_index, hidden, carried_error, q_factor):
    peers = lax.axis_size("expert")
    replicas = lax.axis_size("dp")
    nx = X_CHIPS
    nz = peers // nx
    half = nz // 2
    tokens, model_dim = cotangent.shape[1:]
    capacity, ff = hidden.shape[2:]
    send = capacity // peers
    width = model_dim // PARTS
    vmem = pl.BlockSpec(memory_space=pltpu.VMEM)
    anywhere = pl.BlockSpec(memory_space=pl.ANY)
    dma = pltpu.SemaphoreType.DMA
    rank = q_factor.shape[1]
    share = rank // replicas
    new_error, q_next = pl.pallas_call(
        functools.partial(kernel, nz, nx, send, replicas),
        out_shape=(
            jax.ShapeDtypeStruct((ff, model_dim), bf16),
            jax.ShapeDtypeStruct((rank, model_dim), f32),
        ),
        in_specs=[anywhere] + [vmem] * 3 + [anywhere] * 2 + [vmem],
        out_specs=(vmem, vmem),
        scratch_shapes=[
            pltpu.VMEM((ff, model_dim), f32),
            pltpu.VMEM((3, ff, model_dim), bf16),
            pltpu.VMEM((tokens, model_dim), bf16),
            pltpu.VMEM((2, half, PARTS, tokens, width), bf16),
            pltpu.VMEM((2, half + 1, 16, 128), f32),
            pltpu.VMEM((32, 128), f32),
            pltpu.VMEM((half - 1, PARTS, nx, 2 * send, width), bf16),
            pltpu.VMEM((half - 1, PARTS, nx, 2 * send, width), bf16),
        ]
        + [pltpu.VMEM((PARTS, nx, PAD, width), bf16)] * 4
        + [
            pltpu.VMEM((nz, nx * send, ff), bf16),
            pltpu.VMEM((ff, model_dim), bf16),
        ]
        + [pltpu.VMEM((replicas, share, 1, ff), f32)] * 3
        + [pltpu.VMEM((replicas, share, 1, model_dim), f32)] * 3
        + [
            dma((3,)),
            dma((2, half, PARTS)),
            dma((2, half, PARTS)),
            dma((2, half)),
            dma((2, half)),
            dma((half + 1, PARTS, nx - 1)),
            dma((half + 1, PARTS, nx - 1)),
            dma((4, max(replicas - 1, 1))),
            dma((4, max(replicas - 1, 1))),
        ],
        compiler_params=pltpu.CompilerParams(
            collective_id=0, has_side_effects=True, vmem_limit_bytes=VMEM_BYTES
        ),
        name="route_and_factor",
    )(
        cotangent[0],
        route_weights[0].T,
        expert_ids[0].T,
        slot_index[0].T,
        hidden[0, 0].reshape(nz, nx * send, ff),
        carried_error[0, 0],
        q_factor[0],
    )
    return (new_error[None, None], q_next[None])


def solution(mesh):
    return jax.shard_map(
        shards,
        mesh=mesh,
        in_specs=(
            P("dp", "expert", None),
            P("dp", "expert", None),
            P("dp", "expert", None),
            P("dp", "expert", None),
            P("dp", "expert", None, None),
            P("dp", "expert", None, None),
            P("expert", None, None),
        ),
        out_specs=(P("dp", "expert", None, None), P("expert", None, None)),
        check_vma=False,
    )
```

```python
import functools

import jax
import jax.numpy as jnp
from jax import lax
from jax.experimental import pallas as pl
from jax.experimental.pallas import tpu as pltpu
from jax.sharding import PartitionSpec as P

highest = lax.Precision.HIGHEST
MESH = pl.DeviceIdType.MESH
f32 = jnp.float32
bf16 = jnp.bfloat16

X_CHIPS = 4
PARTS = 4
VMEM_BYTES = 56 * 1024 * 1024
STEPS = 4
PAD = 32


def thirds(value):
    first = value.astype(bf16).astype(f32)
    second = (value - first).astype(bf16).astype(f32)
    return first, second, value - first - second


def kernel(
    nz, nx, send, replicas,
    cot, weights, ids, slots, hidden_hbm, error_hbm, q_rows,
    merged_hbm, basis_stack, q_stack, q_next,
    merged, splits, own, ring, meta, own_meta, picked, arrived, picked_own, arrived_own, picked_far, arrived_far,
    hidden, error,
    left_out, left_in, left_all, right_out, right_in, right_all,
    local_sem, ring_send, ring_recv, meta_send, meta_recv, x_send, x_recv, dp_send, dp_recv,
):
    half = nz // 2
    tokens, model_dim = cot.shape
    width = model_dim // PARTS
    lanes = nx * send
    me = lax.axis_index("expert")
    z = lax.div(me, nx)
    x = lax.rem(me, nx)
    right = lax.rem(z + 1, nz) * nx + x
    left = lax.rem(z + nz - 1, nz) * nx + x
    sides = (right, left)

    load_hidden = pltpu.make_async_copy(hidden_hbm, hidden, local_sem.at[0])
    load_error = pltpu.make_async_copy(error_hbm, error, local_sem.at[1])
    load_own = pltpu.make_async_copy(cot, own, local_sem.at[2])
    load_own.start()

    barrier = pltpu.get_barrier_semaphore()
    partners = [right, left] + [z * nx + lax.rem(x + step, nx) for step in range(1, nx)]
    for partner in partners:
        pl.semaphore_signal(barrier, inc=1, device_id={"expert": partner}, device_id_type=MESH)
    replica = lax.axis_index("dp")
    for step in range(1, replicas):
        partner = lax.rem(replica + step, replicas)
        pl.semaphore_signal(barrier, inc=1, device_id={"dp": partner}, device_id_type=MESH)
    pl.semaphore_wait(barrier, len(partners) + replicas - 1)

    def ring_copy(side, hop, part, source=None):
        return pltpu.make_async_remote_copy(
            src_ref=ring.at[side, hop - 2, part] if source is None else source,
            dst_ref=ring.at[side, hop - 1, part],
            send_sem=ring_send.at[side, hop - 1, part],
            recv_sem=ring_recv.at[side, hop - 1, part],
            device_id={"expert": sides[side]},
            device_id_type=MESH,
        )

    def own_copy(side, part):
        return ring_copy(side, 1, part, own.at[:, pl.ds(part * width, width)])

    def meta_copy(side, hop):
        return pltpu.make_async_remote_copy(
            src_ref=meta.at[side, hop - 1],
            dst_ref=meta.at[side, hop],
            send_sem=meta_send.at[side, hop - 1],
            recv_sem=meta_recv.at[side, hop - 1],
            device_id={"expert": sides[side]},
            device_id_type=MESH,
        )

    def x_copy(pick, land, group, part, step, source=None):
        target = lax.rem(x + step, nx)
        source = x if source is None else source
        return pltpu.make_async_remote_copy(
            src_ref=pick.at[part, target],
            dst_ref=land.at[part, source],
            send_sem=x_send.at[group, part, step - 1],
            recv_sem=x_recv.at[group, part, step - 1],
            device_id={"expert": z * nx + target},
            device_id_type=MESH,
        )

    load_own.wait()
    for part in range(PARTS):
        for side in range(2):
            own_copy(side, part).start()
    load_hidden.start()
    load_error.start()

    routes = ids.shape[0]
    spot = lax.broadcasted_iota(jnp.int32, (128, tokens), 0)
    token = lax.broadcasted_iota(jnp.int32, (128, tokens), 1).astype(f32)
    level = lax.div(ids[...], nx)
    place = lax.rem(ids[...], nx) * send + slots[...]
    to_right = lax.rem(level - z - 1 + 2 * nz, nz)
    to_left = lax.rem(z - level - 1 + 2 * nz, nz) + 16
    table = jnp.zeros((32, 512), f32)
    for k in range(routes):
        row = (spot[:32] == to_right[k : k + 1]) | (spot[:32] == to_left[k : k + 1])
        hit = spot == place[k : k + 1]
        values = [token] + [
            jnp.broadcast_to(v, (128, tokens)) for v in thirds(weights[k : k + 1, :])
        ]
        values = jnp.concatenate([jnp.where(hit, v, 0.0) for v in values], axis=0).astype(bf16)
        table += lax.dot_general(
            jnp.where(row, 1.0, 0.0).astype(bf16), values, (((1,), (1,)), ((), ())),
            preferred_element_type=f32,
        )
    which = table[:, :128]
    gain = (table[:, 384:] + table[:, 256:384]) + table[:, 128:256]
    for side in range(2):
        meta[side, 0, 0:8, :] = which[16 * side : 16 * side + 8]
        meta[side, 0, 8:16, :] = gain[16 * side : 16 * side + 8]
        meta_copy(side, 1).start()
    own_meta[0:16, :] = which[0:16]
    own_meta[16:32, :] = gain[0:16]

    token_lane = lax.broadcasted_iota(jnp.int32, (lanes, tokens), 1).astype(f32)

    def columns(rows):
        stacked = jnp.concatenate(rows + [jnp.zeros((8 - len(rows), 128), f32)], axis=0)
        turned = jnp.transpose(stacked)[:lanes]
        return [turned[:, i : i + 1] for i in range(len(rows))]

    def one_hot(which_column):
        return jnp.where(token_lane == which_column, 1.0, 0.0).astype(bf16)

    def pick_rows(blocks, pick, land, group, part, rows):
        chosen = [
            jnp.dot(choice, block, preferred_element_type=f32) * scale
            for choice, scale, block in blocks
        ]
        pad = rows - send * len(blocks)
        filler = [jnp.zeros((pad, width), f32)] if pad else []
        for target in range(nx):
            cut = [c[target * send : (target + 1) * send] for c in chosen]
            pick[part, target] = jnp.concatenate(cut + filler, axis=0).astype(bf16)
        for step in range(1, nx):
            x_copy(pick, land, group, part, step).start()
        land[part, x] = pick[part, x]

    def hidden_rows(levels, rows):
        blocks = [hidden[v].astype(f32) for v in levels]
        pad = rows - send * len(levels)
        filler = [jnp.zeros((pad, hidden.shape[2]), f32)] if pad else []
        pieces = []
        for source in range(nx):
            pieces += [b[source * send : (source + 1) * send] for b in blocks] + filler
        return jnp.transpose(jnp.concatenate(pieces, axis=0)).astype(bf16)

    def accumulate(land, pick, group, levels, rows, order=range(PARTS), then=None):
        turned = hidden_rows(levels, rows)
        for part in order:
            for step in range(1, nx):
                x_copy(pick, land, group, part, step, lax.rem(x + nx - step, nx)).wait_recv()
            block = land[part].reshape(nx * rows, width)
            merged[:, pl.ds(part * width, width)] += jnp.dot(
                turned, block, preferred_element_type=f32
            )
            if then is not None:
                then(part)

    def pair_levels(hop):
        return [lax.rem(z - hop + nz, nz), lax.rem(z + hop, nz)]

    def step_hop(hop, forward):
        choices = None
        for part in range(PARTS):
            for side in range(2):
                ring_copy(side, hop, part, own.at[:, pl.ds(0, width)]).wait_recv()
                if forward(side, part):
                    ring_copy(side, hop + 1, part).start()
            if choices is None:
                for side in range(2):
                    meta_copy(side, hop).wait_recv()
                    if forward(side, None):
                        meta_copy(side, hop + 1).start()
                got = columns(
                    [meta[s, hop, pl.ds(hop - 1, 1), :] for s in range(2)]
                    + [meta[s, hop, pl.ds(hop + 7, 1), :] for s in range(2)]
                )
                choices = [(one_hot(got[s]), got[2 + s]) for s in range(2)]
            blocks = [choices[s] + (ring[s, hop - 1, part],) for s in range(2)]
            pick_rows(blocks, picked.at[hop - 1], arrived.at[hop - 1], hop - 1, part, 2 * send)

    def add_hop(hop):
        accumulate(arrived.at[hop - 1], picked.at[hop - 1], hop - 1, pair_levels(hop), 2 * send)

    everything = lambda side, part: True
    last = lambda side, part: (side == 0) if part is None else (part < PARTS // 2) == (side == 0)
    def drain_ring(hop, sent=everything):
        for part in range(PARTS):
            for side in range(2):
                if sent(side, part):
                    ring_copy(side, hop, part).wait_send()
        for side in range(2):
            if sent(side, None):
                meta_copy(side, hop).wait_send()

    def drain_x(group, pick=None, land=None):
        pick = picked.at[group] if pick is None else pick
        land = arrived.at[group] if land is None else land
        for part in range(PARTS):
            for step in range(1, nx):
                x_copy(pick, land, group, part, step).wait_send()

    got = columns([own_meta[nz - 1 : nz, :], own_meta[nz + 15 : nz + 16, :]])
    own_choice = (one_hot(got[0]), got[1])
    for part in range(PARTS):
        block = own[:, part * width : (part + 1) * width]
        pick_rows([own_choice + (block,)], picked_own, arrived_own, half - 1, part, PAD)
    load_error.wait()
    merged[...] = error[...].astype(f32)
    load_hidden.wait()

    step_hop(1, everything)
    accumulate(arrived_own, picked_own, half - 1, [z], PAD)
    for part in range(PARTS):
        for side in range(2):
            own_copy(side, part).wait_send()
    for side in range(2):
        meta_copy(side, 1).wait_send()

    def body(hop, carry):
        step_hop(hop, everything)
        add_hop(hop - 1)
        drain_ring(hop)
        drain_x(hop - 2)
        return carry

    lax.fori_loop(2, half - 1, body, 0)
    step_hop(half - 1, last)
    add_hop(half - 2)
    drain_ring(half - 1)
    drain_x(half - 3)

    meta_copy(0, half).wait_recv()
    got = columns([meta[0, half, half - 1 : half, :], meta[0, half, half + 7 : half + 8, :]])
    far_choice = (one_hot(got[0]), got[1])
    order = []
    for part in range(PARTS // 2):
        order += [(0, part), (1, part + PARTS // 2)]
    for side, part in order:
        ring_copy(side, half, part, own.at[:, pl.ds(0, width)]).wait_recv()
        block = ring[side, half - 1, part]
        pick_rows([far_choice + (block,)], picked_far, arrived_far, half, part, PAD)
    add_hop(half - 1)
    far = lax.rem(z + half, nz)
    rank = q_rows.shape[0]
    ff = merged.shape[0]
    q_parts = thirds(q_rows[...])
    blank = jnp.zeros((128 - 3 * rank, model_dim), f32)
    none = jnp.zeros((rank, model_dim), f32)
    q_stacks = [
        jnp.concatenate(list(q_parts[: 3 - i]) + [none] * i + [blank], axis=0).astype(bf16)
        for i in range(3)
    ]
    left_turned = [jnp.zeros((ff, 128), f32)]

    def left_product(part):
        cols = slice(part * width, (part + 1) * width)
        for i, piece in enumerate(thirds(merged[:, cols])):
            piece = piece.astype(bf16)
            splits[i, :, cols] = piece
            left_turned[0] += lax.dot_general(
                piece, q_stacks[i][:, cols], (((1,), (1,)), ((), ())), preferred_element_type=f32
            )

    accumulate(
        arrived_far, picked_far, half, [far], PAD, [part for _, part in order], left_product
    )
    stacked = jnp.transpose(left_turned[0])
    left_local = (stacked[2 * rank : 3 * rank] + stacked[rank : 2 * rank]) + stacked[:rank]

    share = rank // replicas

    def dp_copy(source, target, stage, step, origin):
        return pltpu.make_async_remote_copy(
            src_ref=source,
            dst_ref=target.at[origin],
            send_sem=dp_send.at[stage, step - 1],
            recv_sem=dp_recv.at[stage, step - 1],
            device_id={"dp": lax.rem(replica + step, replicas)},
            device_id_type=MESH,
        )

    def begin_sum(value, out, into, stage):
        for row in range(rank):
            out[row // share, row % share] = value[row : row + 1]
        @pl.loop(1, replicas)
        def _(step):
            target = lax.rem(replica + step, replicas)
            dp_copy(out.at[target], into, stage, step, replica).start()

        into[replica] = out[replica]

    def end_sum(out, into, gathered, stage):
        @pl.loop(1, replicas)
        def _(step):
            origin = lax.rem(replica + replicas - step, replicas)
            dp_copy(out.at[0], into, stage, step, origin).wait_recv()

        total = into[0]
        for origin in range(1, replicas):
            total += into[origin]
        gathered[replica] = total * (1.0 / replicas)

        @pl.loop(1, replicas)
        def _(step):
            dp_copy(gathered.at[replica], gathered, stage + 1, step, replica).start()

    def collect(gathered, stage):
        @pl.loop(1, replicas)
        def _(step):
            origin = lax.rem(replica + replicas - step, replicas)
            dp_copy(gathered.at[replica], gathered, stage + 1, step, origin).wait_recv()

        return jnp.concatenate(
            [gathered[row // share, row % share] for row in range(rank)], axis=0
        )

    begin_sum(left_local, left_out, left_in, 0)
    save_merged = pltpu.make_async_copy(merged, merged_hbm, local_sem.at[3])
    save_merged.start()

    drain_ring(half, last)
    drain_x(half - 2)
    drain_x(half - 1, picked_own, arrived_own)
    drain_x(half, picked_far, arrived_far)

    end_sum(left_out, left_in, left_all, 0)
    left_sum = collect(left_all, 0)

    left_parts = thirds(left_sum)
    left_stack = jnp.concatenate(left_parts, axis=0).astype(bf16)
    right_local = None
    for i in (2, 1, 0):
        product = jnp.dot(left_stack[: (3 - i) * rank], splits[i], preferred_element_type=f32)
        for j in range(2 - i, -1, -1):
            term = product[j * rank : (j + 1) * rank]
            right_local = term if right_local is None else right_local + term
    begin_sum(right_local, right_out, right_in, 2)

    gram = lax.dot_general(
        left_sum, left_sum, (((1,), (1,)), ((), ())),
        precision=highest, preferred_element_type=f32,
    )
    rows = lax.broadcasted_iota(jnp.int32, (rank, rank), 0)
    cols = lax.broadcasted_iota(jnp.int32, (rank, rank), 1)
    row_of = lax.broadcasted_iota(jnp.int32, (rank, 1), 0)
    inverse = jnp.where(rows == cols, 1.0, 0.0)
    pivots = jnp.zeros((rank, 1), f32)
    for k in range(rank):
        pivot = gram[k : k + 1, k : k + 1]
        pivots = jnp.where(row_of == k, pivot, pivots)
        ratio = jnp.where(row_of > k, gram[:, k : k + 1] / pivot, 0.0)
        gram, inverse = gram - ratio * gram[k : k + 1], inverse - ratio * inverse[k : k + 1]
    inverse = inverse / jnp.sqrt(pivots)
    basis = jnp.dot(inverse, left_sum, precision=highest, preferred_element_type=f32)
    b1, b2, b3 = thirds(basis)
    blank = jnp.zeros((128 - 6 * rank, ff), f32)
    basis_stack[...] = jnp.transpose(
        jnp.concatenate([b1, b1, b1, b2, b2, b3, blank], axis=0)
    ).astype(bf16)

    end_sum(right_out, right_in, right_all, 2)
    right_sum = collect(right_all, 2)
    q_new = jnp.dot(inverse, right_sum, precision=highest, preferred_element_type=f32)
    q_next[...] = q_new
    p1, p2, p3 = thirds(q_new)
    blank = jnp.zeros((128 - 6 * rank, model_dim), f32)
    q_stack[...] = jnp.concatenate([p1, p2, p3, p1, p2, p1, blank], axis=0).astype(bf16)
    save_merged.wait()
    for stage, source in enumerate((left_out, left_all, right_out, right_all)):
        @pl.loop(1, replicas)
        def _(step):
            dp_copy(source.at[0], source, stage, step, replica).wait_send()


def apply_kernel(merged, basis_stack, q_stack, q_new, new_error, q_next):
    approx = jnp.dot(basis_stack[...], q_stack[...], preferred_element_type=f32)
    new_error[...] = (merged[...] - approx).astype(bf16)
    q_next[...] = q_new[...]


def shards(cotangent, route_weights, expert_ids, slot_index, hidden, carried_error, q_factor):
    peers = lax.axis_size("expert")
    replicas = lax.axis_size("dp")
    nx = X_CHIPS
    nz = peers // nx
    half = nz // 2
    tokens, model_dim = cotangent.shape[1:]
    capacity, ff = hidden.shape[2:]
    send = capacity // peers
    width = model_dim // PARTS
    vmem = pl.BlockSpec(memory_space=pltpu.VMEM)
    hbm = pl.BlockSpec(memory_space=pltpu.HBM)
    dma = pltpu.SemaphoreType.DMA
    rank = q_factor.shape[1]
    share = rank // replicas
    merged, basis_stack, q_stack, q_new = pl.pallas_call(
        functools.partial(kernel, nz, nx, send, replicas),
        out_shape=(
            jax.ShapeDtypeStruct((ff, model_dim), f32),
            jax.ShapeDtypeStruct((ff, 128), bf16),
            jax.ShapeDtypeStruct((128, model_dim), bf16),
            jax.ShapeDtypeStruct((rank, model_dim), f32),
        ),
        in_specs=[hbm] + [vmem] * 3 + [hbm] * 2 + [vmem],
        out_specs=(hbm, vmem, vmem, vmem),
        scratch_shapes=[
            pltpu.VMEM((ff, model_dim), f32),
            pltpu.VMEM((3, ff, model_dim), bf16),
            pltpu.VMEM((tokens, model_dim), bf16),
            pltpu.VMEM((2, half, PARTS, tokens, width), bf16),
            pltpu.VMEM((2, half + 1, 16, 128), f32),
            pltpu.VMEM((32, 128), f32),
            pltpu.VMEM((half - 1, PARTS, nx, 2 * send, width), bf16),
            pltpu.VMEM((half - 1, PARTS, nx, 2 * send, width), bf16),
        ]
        + [pltpu.VMEM((PARTS, nx, PAD, width), bf16)] * 4
        + [
            pltpu.VMEM((nz, nx * send, ff), bf16),
            pltpu.VMEM((ff, model_dim), bf16),
        ]
        + [pltpu.VMEM((replicas, share, 1, ff), f32)] * 3
        + [pltpu.VMEM((replicas, share, 1, model_dim), f32)] * 3
        + [
            dma((4,)),
            dma((2, half, PARTS)),
            dma((2, half, PARTS)),
            dma((2, half)),
            dma((2, half)),
            dma((half + 1, PARTS, nx - 1)),
            dma((half + 1, PARTS, nx - 1)),
            dma((4, max(replicas - 1, 1))),
            dma((4, max(replicas - 1, 1))),
        ],
        compiler_params=pltpu.CompilerParams(
            collective_id=0, has_side_effects=True, vmem_limit_bytes=VMEM_BYTES
        ),
        name="route_and_factor",
    )(
        cotangent[0],
        route_weights[0].T,
        expert_ids[0].T,
        slot_index[0].T,
        hidden[0, 0].reshape(nz, nx * send, ff),
        carried_error[0, 0],
        q_factor[0],
    )
    rows = ff // STEPS
    new_error, q_next = pl.pallas_call(
        apply_kernel,
        grid=(STEPS,),
        out_shape=(
            jax.ShapeDtypeStruct((ff, model_dim), bf16),
            jax.ShapeDtypeStruct((rank, model_dim), f32),
        ),
        in_specs=[
            pl.BlockSpec((rows, model_dim), lambda i: (i, 0)),
            pl.BlockSpec((rows, 128), lambda i: (i, 0)),
            pl.BlockSpec((128, model_dim), lambda i: (0, 0)),
            pl.BlockSpec((rank, model_dim), lambda i: (0, 0)),
        ],
        out_specs=(
            pl.BlockSpec((rows, model_dim), lambda i: (i, 0)),
            pl.BlockSpec((rank, model_dim), lambda i: (0, 0)),
        ),
        compiler_params=pltpu.CompilerParams(vmem_limit_bytes=VMEM_BYTES),
        name="apply_factors",
    )(merged, basis_stack, q_stack, q_new)
    return (new_error[None, None], q_next[None])


def solution(mesh):
    return jax.shard_map(
        shards,
        mesh=mesh,
        in_specs=(
            P("dp", "expert", None),
            P("dp", "expert", None),
            P("dp", "expert", None),
            P("dp", "expert", None),
            P("dp", "expert", None, None),
            P("dp", "expert", None, None),
            P("expert", None, None),
        ),
        out_specs=(P("dp", "expert", None, None), P("expert", None, None)),
        check_vma=False,
    )
```

```python
import functools

import jax
import jax.numpy as jnp
from jax import lax
from jax.experimental import pallas as pl
from jax.experimental.pallas import tpu as pltpu
from jax.sharding import PartitionSpec as P

highest = lax.Precision.HIGHEST
MESH = pl.DeviceIdType.MESH
f32 = jnp.float32
bf16 = jnp.bfloat16

X_CHIPS = 4
PARTS = 4
VMEM_BYTES = 56 * 1024 * 1024
STEPS = 4
PAD = 32


def thirds(value):
    first = value.astype(bf16).astype(f32)
    second = (value - first).astype(bf16).astype(f32)
    return first, second, value - first - second


def kernel(
    nz, nx, send, replicas,
    cot, weights, ids, slots, hidden_hbm, error_hbm, q_rows,
    merged_hbm, basis_stack, q_stack, q_next,
    merged, splits, own, ring, meta, own_meta, picked, arrived, picked_own, arrived_own, picked_near, arrived_near, direct_out, direct_in,
    hidden, error,
    left_out, left_in, left_all, right_out, right_in, right_all,
    local_sem, ring_send, ring_recv, meta_send, meta_recv, x_send, x_recv,
    direct_send, direct_recv, dp_send, dp_recv,
):
    half = nz // 2
    tokens, model_dim = cot.shape
    width = model_dim // PARTS
    lanes = nx * send
    me = lax.axis_index("expert")
    z = lax.div(me, nx)
    x = lax.rem(me, nx)
    right = lax.rem(z + 1, nz) * nx + x
    left = lax.rem(z + nz - 1, nz) * nx + x
    sides = (right, left)

    load_hidden = pltpu.make_async_copy(hidden_hbm, hidden, local_sem.at[0])
    load_error = pltpu.make_async_copy(error_hbm, error, local_sem.at[1])
    load_own = pltpu.make_async_copy(cot, own, local_sem.at[2])
    load_own.start()

    barrier = pltpu.get_barrier_semaphore()
    levels = (lax.rem(z + 1, nz), lax.rem(z + nz - 1, nz))
    partners = [v * nx + lax.rem(x + step, nx) for step in range(nx) for v in levels]
    partners += [z * nx + lax.rem(x + step, nx) for step in range(1, nx)]
    for partner in partners:
        pl.semaphore_signal(barrier, inc=1, device_id={"expert": partner}, device_id_type=MESH)
    replica = lax.axis_index("dp")
    for step in range(1, replicas):
        partner = lax.rem(replica + step, replicas)
        pl.semaphore_signal(barrier, inc=1, device_id={"dp": partner}, device_id_type=MESH)
    pl.semaphore_wait(barrier, len(partners) + replicas - 1)

    def ring_copy(side, hop, part, source=None):
        return pltpu.make_async_remote_copy(
            src_ref=ring.at[side, hop - 2, part] if source is None else source,
            dst_ref=ring.at[side, hop - 1, part],
            send_sem=ring_send.at[side, hop - 1, part],
            recv_sem=ring_recv.at[side, hop - 1, part],
            device_id={"expert": sides[side]},
            device_id_type=MESH,
        )

    def own_copy(side, part):
        return ring_copy(side, 1, part, own.at[:, pl.ds(part * width, width)])

    def meta_copy(side, hop):
        return pltpu.make_async_remote_copy(
            src_ref=meta.at[side, hop - 1],
            dst_ref=meta.at[side, hop],
            send_sem=meta_send.at[side, hop - 1],
            recv_sem=meta_recv.at[side, hop - 1],
            device_id={"expert": sides[side]},
            device_id_type=MESH,
        )

    def x_copy(pick, land, group, part, step, source=None):
        target = lax.rem(x + step, nx)
        source = x if source is None else source
        return pltpu.make_async_remote_copy(
            src_ref=pick.at[part, target],
            dst_ref=land.at[part, source],
            send_sem=x_send.at[group, part, step - 1],
            recv_sem=x_recv.at[group, part, step - 1],
            device_id={"expert": z * nx + target},
            device_id_type=MESH,
        )

    def direct_copy(stage, side, step, source=None):
        target = lax.rem(x + step, nx)
        source = x if source is None else source
        return pltpu.make_async_remote_copy(
            src_ref=direct_out.at[stage, side, target],
            dst_ref=direct_in.at[stage, side, source],
            send_sem=direct_send.at[stage, side, step],
            recv_sem=direct_recv.at[stage, side, step],
            device_id={"expert": levels[side] * nx + target},
            device_id_type=MESH,
        )

    load_own.wait()
    turn = PARTS // 2
    order = [(part, (part + turn) % PARTS) for part in range(PARTS)]
    kept = (range(turn), range(turn, PARTS))
    for parts in order:
        for side in range(2):
            own_copy(side, parts[side]).start()
    load_hidden.start()
    load_error.start()

    routes = ids.shape[0]
    spot = lax.broadcasted_iota(jnp.int32, (128, tokens), 0)
    token = lax.broadcasted_iota(jnp.int32, (128, tokens), 1).astype(f32)
    level = lax.div(ids[...], nx)
    place = lax.rem(ids[...], nx) * send + slots[...]
    to_right = lax.rem(level - z - 1 + 2 * nz, nz)
    to_left = lax.rem(z - level - 1 + 2 * nz, nz) + 16
    table = jnp.zeros((32, 512), f32)
    for k in range(routes):
        row = (spot[:32] == to_right[k : k + 1]) | (spot[:32] == to_left[k : k + 1])
        hit = spot == place[k : k + 1]
        values = [token] + [
            jnp.broadcast_to(v, (128, tokens)) for v in thirds(weights[k : k + 1, :])
        ]
        values = jnp.concatenate([jnp.where(hit, v, 0.0) for v in values], axis=0).astype(bf16)
        table += lax.dot_general(
            jnp.where(row, 1.0, 0.0).astype(bf16), values, (((1,), (1,)), ((), ())),
            preferred_element_type=f32,
        )
    which = table[:, :128]
    gain = (table[:, 384:] + table[:, 256:384]) + table[:, 128:256]
    for side in range(2):
        meta[side, 0, 0:8, :] = which[16 * side : 16 * side + 8]
        meta[side, 0, 8:16, :] = gain[16 * side : 16 * side + 8]
        meta_copy(side, 1).start()
    own_meta[0:16, :] = which[0:16]
    own_meta[16:32, :] = gain[0:16]

    token_lane = lax.broadcasted_iota(jnp.int32, (lanes, tokens), 1).astype(f32)

    def columns(rows):
        stacked = jnp.concatenate(rows + [jnp.zeros((8 - len(rows), 128), f32)], axis=0)
        turned = jnp.transpose(stacked)[:lanes]
        return [turned[:, i : i + 1] for i in range(len(rows))]

    def one_hot(which_column):
        return jnp.where(token_lane == which_column, 1.0, 0.0).astype(bf16)

    def pick_rows(blocks, pick, rows):
        chosen = [
            jnp.dot(choice, block, preferred_element_type=f32) * scale
            for choice, scale, block in blocks
        ]
        pad = rows - send * len(blocks)
        filler = [jnp.zeros((pad, width), f32)] if pad else []
        for target in range(nx):
            cut = [c[target * send : (target + 1) * send] for c in chosen]
            pick[target] = jnp.concatenate(cut + filler, axis=0).astype(bf16)

    def pass_rows(pick, land, group, part):
        for step in range(1, nx):
            x_copy(pick, land, group, part, step).start()
        land[part, x] = pick[part, x]

    def choices_of(hop, distance):
        got = columns(
            [meta[s, hop, pl.ds(distance - 1, 1), :] for s in range(2)]
            + [meta[s, hop, pl.ds(distance + 7, 1), :] for s in range(2)]
        )
        return [(one_hot(got[s]), got[2 + s]) for s in range(2)]

    def hidden_rows(levels, rows):
        blocks = [hidden[v].astype(f32) for v in levels]
        pad = rows - send * len(levels)
        filler = [jnp.zeros((pad, hidden.shape[2]), f32)] if pad else []
        pieces = []
        for source in range(nx):
            pieces += [b[source * send : (source + 1) * send] for b in blocks] + filler
        return jnp.transpose(jnp.concatenate(pieces, axis=0)).astype(bf16)

    def accumulate(land, pick, group, levels, rows):
        turned = hidden_rows(levels, rows)
        for part in range(PARTS):
            for step in range(1, nx):
                x_copy(pick, land, group, part, step, lax.rem(x + nx - step, nx)).wait_recv()
            block = land[part].reshape(nx * rows, width)
            merged[:, pl.ds(part * width, width)] += jnp.dot(
                turned, block, preferred_element_type=f32
            )

    def pair_levels(hop):
        return [lax.rem(z - hop + nz, nz), lax.rem(z + hop, nz)]

    def step_hop(hop, forward):
        choices = None
        for slot, parts in enumerate(order):
            for side in range(2):
                ring_copy(side, hop, parts[side], own.at[:, pl.ds(0, width)]).wait_recv()
                if forward(side, parts[side]):
                    ring_copy(side, hop + 1, parts[side]).start()
            if choices is None:
                for side in range(2):
                    meta_copy(side, hop).wait_recv()
                    meta_copy(side, hop + 1).start()
                choices = choices_of(hop, hop)
            if slot >= turn:
                for part in parts:
                    blocks = [choices[s] + (ring[s, hop - 1, part],) for s in range(2)]
                    pick_rows(blocks, picked.at[hop - 1, part], 2 * send)
                    pass_rows(picked.at[hop - 1], arrived.at[hop - 1], hop - 1, part)

    def send_direct(stage, hop):
        choices = choices_of(hop, hop + 1)
        for side in range(2):
            parts = kept[side] if stage else kept[1 - side]
            blocks = [choices[side] + (ring[side, hop - 1, part],) for part in parts]
            pick_rows(blocks, direct_out.at[stage, side], 2 * send)
            for step in range(nx):
                direct_copy(stage, side, step).start()

    def add_hop(hop):
        accumulate(arrived.at[hop - 1], picked.at[hop - 1], hop - 1, pair_levels(hop), 2 * send)

    everything = lambda side, part: True
    going_on = lambda side, part: part in kept[side]

    def drain_ring(hop, sent=everything):
        for part in range(PARTS):
            for side in range(2):
                if sent(side, part):
                    ring_copy(side, hop, part).wait_send()
        for side in range(2):
            meta_copy(side, hop).wait_send()

    def drain_x(group, pick, land, parts=range(PARTS)):
        for part in parts:
            for step in range(1, nx):
                x_copy(pick, land, group, part, step).wait_send()

    def drain_hop(hop):
        drain_x(hop - 1, picked.at[hop - 1], arrived.at[hop - 1])

    got = columns([own_meta[nz - 1 : nz, :], own_meta[nz + 15 : nz + 16, :]])
    own_choice = (one_hot(got[0]), got[1])
    for part in range(PARTS):
        block = own[:, part * width : (part + 1) * width]
        pick_rows([own_choice + (block,)], picked_own.at[part], PAD)
        pass_rows(picked_own, arrived_own, half - 2, part)
    load_error.wait()
    merged[...] = error[...].astype(f32)
    load_hidden.wait()

    step_hop(1, everything)
    accumulate(arrived_own, picked_own, half - 2, [z], PAD)
    for part in range(PARTS):
        for side in range(2):
            own_copy(side, part).wait_send()
    for side in range(2):
        meta_copy(side, 1).wait_send()
    drain_x(half - 2, picked_own, arrived_own)

    def body(hop, carry):
        step_hop(hop, everything)
        add_hop(hop - 1)
        drain_ring(hop)
        drain_hop(hop - 1)
        return carry

    lax.fori_loop(2, half - 2, body, 0)
    step_hop(half - 2, going_on)
    send_direct(0, half - 2)
    add_hop(half - 3)
    drain_ring(half - 2)
    drain_hop(half - 3)

    for parts in order[:turn]:
        for side in range(2):
            ring_copy(side, half - 1, parts[side], own.at[:, pl.ds(0, width)]).wait_recv()
    for side in range(2):
        meta_copy(side, half - 1).wait_recv()
    send_direct(1, half - 1)
    choices = choices_of(half - 1, half - 1)
    for side in range(2):
        blocks = [choices[side] + (ring[side, half - 2, part],) for part in kept[side]]
        pick_rows(blocks, picked_near.at[side], 2 * send)
        pass_rows(picked_near, arrived_near, half - 1, side)
    add_hop(half - 2)
    drain_ring(half - 1, going_on)
    drain_hop(half - 2)

    def stacked_rows(level):
        block = hidden[level].astype(f32)
        pieces = [block[source * send : (source + 1) * send] for source in range(nx)]
        gap = jnp.zeros((send, hidden.shape[2]), f32)
        first = jnp.concatenate([p for piece in pieces for p in (piece, gap)], axis=0)
        second = jnp.concatenate([p for piece in pieces for p in (gap, piece)], axis=0)
        return [jnp.transpose(v).astype(bf16) for v in (first, second)]

    def product(lhs, buffer):
        rows = buffer.reshape(nx * 2 * send, width)
        return jnp.dot(lhs, rows, preferred_element_type=f32)

    before, after = pair_levels(half - 1)
    lhs_sides = [stacked_rows(before), stacked_rows(after)]
    lhs_far = stacked_rows(lax.rem(z + half, nz))
    for side in range(2):
        for step in range(1, nx):
            origin = lax.rem(x + nx - step, nx)
            x_copy(picked_near, arrived_near, half - 1, side, step, origin).wait_recv()
    for side in range(2):
        for step in range(nx):
            direct_copy(0, side, step, lax.rem(x + nx - step, nx)).wait_recv()
    for side in range(2):
        for index, part in enumerate(kept[side]):
            merged[:, part * width : (part + 1) * width] += product(
                lhs_sides[side][index], arrived_near[side]
            ) + product(lhs_sides[1 - side][index], direct_in[0, 1 - side])

    rank = q_rows.shape[0]
    ff = merged.shape[0]
    q_parts = thirds(q_rows[...])
    blank = jnp.zeros((128 - 3 * rank, model_dim), f32)
    none = jnp.zeros((rank, model_dim), f32)
    q_stacks = [
        jnp.concatenate(list(q_parts[: 3 - i]) + [none] * i + [blank], axis=0).astype(bf16)
        for i in range(3)
    ]
    left_turned = [jnp.zeros((ff, 128), f32)]

    def left_product(part):
        cols = slice(part * width, (part + 1) * width)
        for i, piece in enumerate(thirds(merged[:, cols])):
            piece = piece.astype(bf16)
            splits[i, :, cols] = piece
            left_turned[0] += lax.dot_general(
                piece, q_stacks[i][:, cols], (((1,), (1,)), ((), ())), preferred_element_type=f32
            )

    for side in range(2):
        for step in range(nx):
            direct_copy(1, side, step, lax.rem(x + nx - step, nx)).wait_recv()
        for index, part in enumerate(kept[side]):
            merged[:, part * width : (part + 1) * width] += product(
                lhs_far[index], direct_in[1, side]
            )
            left_product(part)
    stacked = jnp.transpose(left_turned[0])
    left_local = (stacked[2 * rank : 3 * rank] + stacked[rank : 2 * rank]) + stacked[:rank]

    share = rank // replicas

    def dp_copy(source, target, stage, step, origin):
        return pltpu.make_async_remote_copy(
            src_ref=source,
            dst_ref=target.at[origin],
            send_sem=dp_send.at[stage, step - 1],
            recv_sem=dp_recv.at[stage, step - 1],
            device_id={"dp": lax.rem(replica + step, replicas)},
            device_id_type=MESH,
        )

    def begin_sum(value, out, into, stage):
        for row in range(rank):
            out[row // share, row % share] = value[row : row + 1]
        @pl.loop(1, replicas)
        def _(step):
            target = lax.rem(replica + step, replicas)
            dp_copy(out.at[target], into, stage, step, replica).start()

        into[replica] = out[replica]

    def end_sum(out, into, gathered, stage):
        @pl.loop(1, replicas)
        def _(step):
            origin = lax.rem(replica + replicas - step, replicas)
            dp_copy(out.at[0], into, stage, step, origin).wait_recv()

        total = into[0]
        for origin in range(1, replicas):
            total += into[origin]
        gathered[replica] = total * (1.0 / replicas)

        @pl.loop(1, replicas)
        def _(step):
            dp_copy(gathered.at[replica], gathered, stage + 1, step, replica).start()

    def collect(gathered, stage):
        @pl.loop(1, replicas)
        def _(step):
            origin = lax.rem(replica + replicas - step, replicas)
            dp_copy(gathered.at[replica], gathered, stage + 1, step, origin).wait_recv()

        return jnp.concatenate(
            [gathered[row // share, row % share] for row in range(rank)], axis=0
        )

    begin_sum(left_local, left_out, left_in, 0)
    save_merged = pltpu.make_async_copy(merged, merged_hbm, local_sem.at[3])
    save_merged.start()

    drain_x(half - 1, picked_near, arrived_near, range(2))
    for stage in range(2):
        for side in range(2):
            for step in range(nx):
                direct_copy(stage, side, step).wait_send()

    end_sum(left_out, left_in, left_all, 0)
    left_sum = collect(left_all, 0)

    left_parts = thirds(left_sum)
    left_stack = jnp.concatenate(left_parts, axis=0).astype(bf16)
    right_local = None
    for i in (2, 1, 0):
        product = jnp.dot(left_stack[: (3 - i) * rank], splits[i], preferred_element_type=f32)
        for j in range(2 - i, -1, -1):
            term = product[j * rank : (j + 1) * rank]
            right_local = term if right_local is None else right_local + term
    begin_sum(right_local, right_out, right_in, 2)

    gram = lax.dot_general(
        left_sum, left_sum, (((1,), (1,)), ((), ())),
        precision=highest, preferred_element_type=f32,
    )
    rows = lax.broadcasted_iota(jnp.int32, (rank, rank), 0)
    cols = lax.broadcasted_iota(jnp.int32, (rank, rank), 1)
    row_of = lax.broadcasted_iota(jnp.int32, (rank, 1), 0)
    inverse = jnp.where(rows == cols, 1.0, 0.0)
    pivots = jnp.zeros((rank, 1), f32)
    for k in range(rank):
        pivot = gram[k : k + 1, k : k + 1]
        pivots = jnp.where(row_of == k, pivot, pivots)
        ratio = jnp.where(row_of > k, gram[:, k : k + 1] / pivot, 0.0)
        gram, inverse = gram - ratio * gram[k : k + 1], inverse - ratio * inverse[k : k + 1]
    inverse = inverse / jnp.sqrt(pivots)
    basis = jnp.dot(inverse, left_sum, precision=highest, preferred_element_type=f32)
    b1, b2, b3 = thirds(basis)
    blank = jnp.zeros((128 - 6 * rank, ff), f32)
    basis_stack[...] = jnp.transpose(
        jnp.concatenate([b1, b1, b1, b2, b2, b3, blank], axis=0)
    ).astype(bf16)

    end_sum(right_out, right_in, right_all, 2)
    right_sum = collect(right_all, 2)
    q_new = jnp.dot(inverse, right_sum, precision=highest, preferred_element_type=f32)
    q_next[...] = q_new
    p1, p2, p3 = thirds(q_new)
    blank = jnp.zeros((128 - 6 * rank, model_dim), f32)
    q_stack[...] = jnp.concatenate([p1, p2, p3, p1, p2, p1, blank], axis=0).astype(bf16)
    save_merged.wait()
    for stage, source in enumerate((left_out, left_all, right_out, right_all)):
        @pl.loop(1, replicas)
        def _(step):
            dp_copy(source.at[0], source, stage, step, replica).wait_send()


def apply_kernel(
    merged_hbm, basis_hbm, stack_hbm, q_hbm, error_hbm, next_hbm,
    merged, basis_stack, q_stack, new_error, load_sem, small_sem, store_sem,
):
    rows = merged.shape[1]
    small = [
        pltpu.make_async_copy(basis_hbm, basis_stack, small_sem.at[0]),
        pltpu.make_async_copy(stack_hbm, q_stack, small_sem.at[1]),
        pltpu.make_async_copy(q_hbm, next_hbm, small_sem.at[2]),
    ]
    loads = [
        pltpu.make_async_copy(merged_hbm.at[pl.ds(i * rows, rows)], merged.at[i], load_sem.at[i])
        for i in range(STEPS)
    ]
    stores = [
        pltpu.make_async_copy(new_error.at[i], error_hbm.at[pl.ds(i * rows, rows)], store_sem.at[i])
        for i in range(STEPS)
    ]
    for copy in small + loads:
        copy.start()
    small[0].wait()
    small[1].wait()
    for i in range(STEPS):
        loads[i].wait()
        approx = jnp.dot(
            basis_stack[i * rows : (i + 1) * rows], q_stack[...], preferred_element_type=f32
        )
        new_error[i] = (merged[i] - approx).astype(bf16)
        stores[i].start()
    small[2].wait()
    for copy in stores:
        copy.wait()


def shards(cotangent, route_weights, expert_ids, slot_index, hidden, carried_error, q_factor):
    peers = lax.axis_size("expert")
    replicas = lax.axis_size("dp")
    nx = X_CHIPS
    nz = peers // nx
    half = nz // 2
    tokens, model_dim = cotangent.shape[1:]
    capacity, ff = hidden.shape[2:]
    send = capacity // peers
    width = model_dim // PARTS
    vmem = pl.BlockSpec(memory_space=pltpu.VMEM)
    hbm = pl.BlockSpec(memory_space=pltpu.HBM)
    dma = pltpu.SemaphoreType.DMA
    rank = q_factor.shape[1]
    share = rank // replicas
    merged, basis_stack, q_stack, q_new = pl.pallas_call(
        functools.partial(kernel, nz, nx, send, replicas),
        out_shape=(
            jax.ShapeDtypeStruct((ff, model_dim), f32),
            jax.ShapeDtypeStruct((ff, 128), bf16),
            jax.ShapeDtypeStruct((128, model_dim), bf16),
            jax.ShapeDtypeStruct((rank, model_dim), f32),
        ),
        in_specs=[hbm] + [vmem] * 3 + [hbm] * 2 + [vmem],
        out_specs=(hbm, vmem, vmem, vmem),
        scratch_shapes=[
            pltpu.VMEM((ff, model_dim), f32),
            pltpu.VMEM((3, ff, model_dim), bf16),
            pltpu.VMEM((tokens, model_dim), bf16),
            pltpu.VMEM((2, half - 1, PARTS, tokens, width), bf16),
            pltpu.VMEM((2, half, 16, 128), f32),
            pltpu.VMEM((32, 128), f32),
            pltpu.VMEM((half - 2, PARTS, nx, 2 * send, width), bf16),
            pltpu.VMEM((half - 2, PARTS, nx, 2 * send, width), bf16),
        ]
        + [pltpu.VMEM((PARTS, nx, PAD, width), bf16)] * 2
        + [pltpu.VMEM((2, nx, 2 * send, width), bf16)] * 2
        + [pltpu.VMEM((2, 2, nx, 2 * send, width), bf16)] * 2
        + [
            pltpu.VMEM((nz, nx * send, ff), bf16),
            pltpu.VMEM((ff, model_dim), bf16),
        ]
        + [pltpu.VMEM((replicas, share, 1, ff), f32)] * 3
        + [pltpu.VMEM((replicas, share, 1, model_dim), f32)] * 3
        + [
            dma((4,)),
            dma((2, half - 1, PARTS)),
            dma((2, half - 1, PARTS)),
            dma((2, half - 1)),
            dma((2, half - 1)),
            dma((half, PARTS, nx - 1)),
            dma((half, PARTS, nx - 1)),
            dma((2, 2, nx)),
            dma((2, 2, nx)),
            dma((4, max(replicas - 1, 1))),
            dma((4, max(replicas - 1, 1))),
        ],
        compiler_params=pltpu.CompilerParams(
            collective_id=0, has_side_effects=True, vmem_limit_bytes=VMEM_BYTES
        ),
        name="route_and_factor",
    )(
        cotangent[0],
        route_weights[0].T,
        expert_ids[0].T,
        slot_index[0].T,
        hidden[0, 0].reshape(nz, nx * send, ff),
        carried_error[0, 0],
        q_factor[0],
    )
    rows = ff // STEPS
    new_error, q_next = pl.pallas_call(
        apply_kernel,
        out_shape=(
            jax.ShapeDtypeStruct((ff, model_dim), bf16),
            jax.ShapeDtypeStruct((rank, model_dim), f32),
        ),
        in_specs=[hbm] * 4,
        out_specs=(hbm, hbm),
        scratch_shapes=[
            pltpu.VMEM((STEPS, rows, model_dim), f32),
            pltpu.VMEM((ff, 128), bf16),
            pltpu.VMEM((128, model_dim), bf16),
            pltpu.VMEM((STEPS, rows, model_dim), bf16),
            dma((STEPS,)),
            dma((3,)),
            dma((STEPS,)),
        ],
        compiler_params=pltpu.CompilerParams(vmem_limit_bytes=VMEM_BYTES),
        name="apply_factors",
    )(merged, basis_stack, q_stack, q_new)
    return (new_error[None, None], q_next[None])


def solution(mesh):
    return jax.shard_map(
        shards,
        mesh=mesh,
        in_specs=(
            P("dp", "expert", None),
            P("dp", "expert", None),
            P("dp", "expert", None),
            P("dp", "expert", None),
            P("dp", "expert", None, None),
            P("dp", "expert", None, None),
            P("expert", None, None),
        ),
        out_specs=(P("dp", "expert", None, None), P("expert", None, None)),
        check_vma=False,
    )
```

```python
import functools

import jax
import jax.numpy as jnp
from jax import lax
from jax.experimental import pallas as pl
from jax.experimental.pallas import tpu as pltpu
from jax.sharding import PartitionSpec as P

highest = lax.Precision.HIGHEST
MESH = pl.DeviceIdType.MESH
f32 = jnp.float32
bf16 = jnp.bfloat16

X_CHIPS = 4
PARTS = 4
VMEM_BYTES = 56 * 1024 * 1024
STEPS = 4
PAD = 32


def thirds(value):
    first = value.astype(bf16).astype(f32)
    second = (value - first).astype(bf16).astype(f32)
    return first, second, value - first - second


def halves(value):
    first = value.astype(bf16).astype(f32)
    return first, value - first


def kernel(
    nz, nx, send, replicas,
    cot, weights_hbm, ids_hbm, slots_hbm, hidden_hbm, error_hbm, q_hbm,
    merged_hbm, basis_hbm, q_next,
    weights, ids, slots, q_rows, basis_stack, merged, splits, own, ring, meta, own_meta, picked, arrived, picked_own, arrived_own, picked_near, arrived_near, direct_out, direct_in,
    hidden, error,
    left_out, left_in, left_all, right_out, right_in, right_all,
    local_sem, small_sem, ring_send, ring_recv, meta_send, meta_recv, x_send, x_recv,
    direct_send, direct_recv, dp_send, dp_recv,
):
    half = nz // 2
    tokens, model_dim = cot.shape
    width = model_dim // PARTS
    lanes = nx * send
    me = lax.axis_index("expert")
    z = lax.div(me, nx)
    x = lax.rem(me, nx)
    right = lax.rem(z + 1, nz) * nx + x
    left = lax.rem(z + nz - 1, nz) * nx + x
    sides = (right, left)

    load_hidden = pltpu.make_async_copy(hidden_hbm, hidden, local_sem.at[0])
    load_error = pltpu.make_async_copy(error_hbm, error, local_sem.at[1])
    load_own = pltpu.make_async_copy(cot, own, local_sem.at[2])
    load_own.start()
    load_small = [
        pltpu.make_async_copy(source, target, small_sem.at[i])
        for i, (source, target) in enumerate(
            ((ids_hbm, ids), (slots_hbm, slots), (weights_hbm, weights), (q_hbm, q_rows))
        )
    ]
    for load in load_small:
        load.start()

    barrier = pltpu.get_barrier_semaphore()
    levels = (lax.rem(z + 1, nz), lax.rem(z + nz - 1, nz))
    partners = [v * nx + lax.rem(x + step, nx) for step in range(nx) for v in levels]
    partners += [z * nx + lax.rem(x + step, nx) for step in range(1, nx)]
    for partner in partners:
        pl.semaphore_signal(barrier, inc=1, device_id={"expert": partner}, device_id_type=MESH)
    replica = lax.axis_index("dp")
    for step in range(1, replicas):
        partner = lax.rem(replica + step, replicas)
        pl.semaphore_signal(barrier, inc=1, device_id={"dp": partner}, device_id_type=MESH)
    pl.semaphore_wait(barrier, len(partners) + replicas - 1)

    def ring_copy(side, hop, part, source=None):
        return pltpu.make_async_remote_copy(
            src_ref=ring.at[side, hop - 2, part] if source is None else source,
            dst_ref=ring.at[side, hop - 1, part],
            send_sem=ring_send.at[side, hop - 1, part],
            recv_sem=ring_recv.at[side, hop - 1, part],
            device_id={"expert": sides[side]},
            device_id_type=MESH,
        )

    def own_copy(side, part):
        return ring_copy(side, 1, part, own.at[:, pl.ds(part * width, width)])

    def meta_copy(side, hop):
        return pltpu.make_async_remote_copy(
            src_ref=meta.at[side, hop - 1],
            dst_ref=meta.at[side, hop],
            send_sem=meta_send.at[side, hop - 1],
            recv_sem=meta_recv.at[side, hop - 1],
            device_id={"expert": sides[side]},
            device_id_type=MESH,
        )

    def x_copy(pick, land, group, part, step, source=None):
        target = lax.rem(x + step, nx)
        source = x if source is None else source
        return pltpu.make_async_remote_copy(
            src_ref=pick.at[part, target],
            dst_ref=land.at[part, source],
            send_sem=x_send.at[group, part, step - 1],
            recv_sem=x_recv.at[group, part, step - 1],
            device_id={"expert": z * nx + target},
            device_id_type=MESH,
        )

    def direct_copy(stage, side, step, source=None):
        target = lax.rem(x + step, nx)
        source = x if source is None else source
        return pltpu.make_async_remote_copy(
            src_ref=direct_out.at[stage, side, target],
            dst_ref=direct_in.at[stage, side, source],
            send_sem=direct_send.at[stage, side, step],
            recv_sem=direct_recv.at[stage, side, step],
            device_id={"expert": levels[side] * nx + target},
            device_id_type=MESH,
        )

    load_own.wait()
    turn = PARTS // 2
    order = [(part, (part + turn) % PARTS) for part in range(PARTS)]
    kept = (range(turn), range(turn, PARTS))
    for parts in order:
        for side in range(2):
            own_copy(side, parts[side]).start()
    load_hidden.start()
    load_error.start()

    for load in load_small:
        load.wait()
    routes = ids.shape[0]
    spot = lax.broadcasted_iota(jnp.int32, (128, tokens), 0)
    token = lax.broadcasted_iota(jnp.int32, (128, tokens), 1).astype(f32)
    level = lax.div(ids[...], nx)
    place = lax.rem(ids[...], nx) * send + slots[...]
    to_right = lax.rem(level - z - 1 + 2 * nz, nz)
    to_left = lax.rem(z - level - 1 + 2 * nz, nz) + 16
    table = jnp.zeros((32, 512), f32)
    for k in range(routes):
        row = (spot[:32] == to_right[k : k + 1]) | (spot[:32] == to_left[k : k + 1])
        hit = spot == place[k : k + 1]
        values = [token] + [
            jnp.broadcast_to(v, (128, tokens)) for v in thirds(weights[k : k + 1, :])
        ]
        values = jnp.concatenate([jnp.where(hit, v, 0.0) for v in values], axis=0).astype(bf16)
        table += lax.dot_general(
            jnp.where(row, 1.0, 0.0).astype(bf16), values, (((1,), (1,)), ((), ())),
            preferred_element_type=f32,
        )
    which = table[:, :128]
    gain = (table[:, 384:] + table[:, 256:384]) + table[:, 128:256]
    for side in range(2):
        meta[side, 0, 0:8, :] = which[16 * side : 16 * side + 8]
        meta[side, 0, 8:16, :] = gain[16 * side : 16 * side + 8]
        meta_copy(side, 1).start()
    own_meta[0:16, :] = which[0:16]
    own_meta[16:32, :] = gain[0:16]

    token_lane = lax.broadcasted_iota(jnp.int32, (lanes, tokens), 1).astype(f32)

    def columns(rows):
        stacked = jnp.concatenate(rows + [jnp.zeros((8 - len(rows), 128), f32)], axis=0)
        turned = jnp.transpose(stacked)[:lanes]
        return [turned[:, i : i + 1] for i in range(len(rows))]

    def one_hot(which_column):
        return jnp.where(token_lane == which_column, 1.0, 0.0).astype(bf16)

    def pick_rows(blocks, pick, rows):
        chosen = [
            jnp.dot(choice, block, preferred_element_type=f32) * scale
            for choice, scale, block in blocks
        ]
        pad = rows - send * len(blocks)
        filler = [jnp.zeros((pad, width), f32)] if pad else []
        for target in range(nx):
            cut = [c[target * send : (target + 1) * send] for c in chosen]
            pick[target] = jnp.concatenate(cut + filler, axis=0).astype(bf16)

    def pass_rows(pick, land, group, part):
        for step in range(1, nx):
            x_copy(pick, land, group, part, step).start()
        land[part, x] = pick[part, x]

    def choices_of(hop, distance):
        got = columns(
            [meta[s, hop, pl.ds(distance - 1, 1), :] for s in range(2)]
            + [meta[s, hop, pl.ds(distance + 7, 1), :] for s in range(2)]
        )
        return [(one_hot(got[s]), got[2 + s]) for s in range(2)]

    def hidden_rows(levels, rows):
        blocks = [hidden[v].astype(f32) for v in levels]
        pad = rows - send * len(levels)
        filler = [jnp.zeros((pad, hidden.shape[2]), f32)] if pad else []
        pieces = []
        for source in range(nx):
            pieces += [b[source * send : (source + 1) * send] for b in blocks] + filler
        return jnp.transpose(jnp.concatenate(pieces, axis=0)).astype(bf16)

    def accumulate(land, pick, group, turned, rows, parts):
        for part in parts:
            for step in range(1, nx):
                x_copy(pick, land, group, part, step, lax.rem(x + nx - step, nx)).wait_recv()
            block = land[part].reshape(nx * rows, width)
            merged[:, pl.ds(part * width, width)] += jnp.dot(
                turned, block, preferred_element_type=f32
            )

    def pair_levels(hop):
        return [lax.rem(z - hop + nz, nz), lax.rem(z + hop, nz)]

    def step_hop(hop, forward, add):
        choices = None
        for slot, parts in enumerate(order):
            for side in range(2):
                ring_copy(side, hop, parts[side], own.at[:, pl.ds(0, width)]).wait_recv()
                if forward(side, parts[side]):
                    ring_copy(side, hop + 1, parts[side]).start()
            if choices is None:
                for side in range(2):
                    meta_copy(side, hop).wait_recv()
                    meta_copy(side, hop + 1).start()
                choices = choices_of(hop, hop)
            if slot < turn:
                add(parts)
            else:
                for part in parts:
                    blocks = [choices[s] + (ring[s, hop - 1, part],) for s in range(2)]
                    pick_rows(blocks, picked.at[hop - 1, part], 2 * send)
                    pass_rows(picked.at[hop - 1], arrived.at[hop - 1], hop - 1, part)

    def send_direct(stage, hop):
        choices = choices_of(hop, hop + 1)
        for side in range(2):
            parts = kept[side] if stage else kept[1 - side]
            blocks = [choices[side] + (ring[side, hop - 1, part],) for part in parts]
            pick_rows(blocks, direct_out.at[stage, side], 2 * send)
            for step in range(nx):
                direct_copy(stage, side, step).start()

    def adder(hop):
        turned = hidden_rows(pair_levels(hop), 2 * send)
        group = hop - 1

        def add(parts):
            accumulate(arrived.at[group], picked.at[group], group, turned, 2 * send, parts)

        return add

    everything = lambda side, part: True
    going_on = lambda side, part: part in kept[side]

    def drain_ring(hop, sent=everything):
        for part in range(PARTS):
            for side in range(2):
                if sent(side, part):
                    ring_copy(side, hop, part).wait_send()
        for side in range(2):
            meta_copy(side, hop).wait_send()

    def drain_x(group, pick, land, parts=range(PARTS)):
        for part in parts:
            for step in range(1, nx):
                x_copy(pick, land, group, part, step).wait_send()

    def drain_hop(hop):
        drain_x(hop - 1, picked.at[hop - 1], arrived.at[hop - 1])

    got = columns([own_meta[nz - 1 : nz, :], own_meta[nz + 15 : nz + 16, :]])
    own_choice = (one_hot(got[0]), got[1])
    for part in range(PARTS):
        block = own[:, part * width : (part + 1) * width]
        pick_rows([own_choice + (block,)], picked_own.at[part], PAD)
        pass_rows(picked_own, arrived_own, half - 2, part)
    load_error.wait()
    merged[...] = error[...].astype(f32)
    load_hidden.wait()

    turned_own = hidden_rows([z], PAD)
    add_own = lambda parts: accumulate(
        arrived_own, picked_own, half - 2, turned_own, PAD, parts
    )
    step_hop(1, everything, add_own)
    for part in range(PARTS):
        for side in range(2):
            own_copy(side, part).wait_send()
    for side in range(2):
        meta_copy(side, 1).wait_send()
    drain_x(half - 2, picked_own, arrived_own)

    def body(hop, carry):
        step_hop(hop, everything, adder(hop - 1))
        drain_ring(hop)
        drain_hop(hop - 1)
        return carry

    lax.fori_loop(2, half - 2, body, 0)
    step_hop(half - 2, going_on, adder(half - 3))
    send_direct(0, half - 2)
    drain_ring(half - 2)
    drain_hop(half - 3)

    for parts in order[:turn]:
        for side in range(2):
            ring_copy(side, half - 1, parts[side], own.at[:, pl.ds(0, width)]).wait_recv()
    for side in range(2):
        meta_copy(side, half - 1).wait_recv()
    send_direct(1, half - 1)
    choices = choices_of(half - 1, half - 1)
    for side in range(2):
        blocks = [choices[side] + (ring[side, half - 2, part],) for part in kept[side]]
        pick_rows(blocks, picked_near.at[side], 2 * send)
        pass_rows(picked_near, arrived_near, half - 1, side)
    adder(half - 2)(range(PARTS))
    drain_ring(half - 1, going_on)
    drain_hop(half - 2)

    def stacked_rows(level):
        block = hidden[level].astype(f32)
        pieces = [block[source * send : (source + 1) * send] for source in range(nx)]
        gap = jnp.zeros((send, hidden.shape[2]), f32)
        first = jnp.concatenate([p for piece in pieces for p in (piece, gap)], axis=0)
        second = jnp.concatenate([p for piece in pieces for p in (gap, piece)], axis=0)
        return [jnp.transpose(v).astype(bf16) for v in (first, second)]

    def product(lhs, buffer):
        rows = buffer.reshape(nx * 2 * send, width)
        return jnp.dot(lhs, rows, preferred_element_type=f32)

    before, after = pair_levels(half - 1)
    lhs_sides = [stacked_rows(before), stacked_rows(after)]
    lhs_far = stacked_rows(lax.rem(z + half, nz))
    for side in range(2):
        for step in range(1, nx):
            origin = lax.rem(x + nx - step, nx)
            x_copy(picked_near, arrived_near, half - 1, side, step, origin).wait_recv()
    for side in range(2):
        for step in range(nx):
            direct_copy(0, side, step, lax.rem(x + nx - step, nx)).wait_recv()
    for side in range(2):
        for index, part in enumerate(kept[side]):
            merged[:, part * width : (part + 1) * width] += product(
                lhs_sides[side][index], arrived_near[side]
            ) + product(lhs_sides[1 - side][index], direct_in[0, 1 - side])

    rank = q_rows.shape[0]
    ff = merged.shape[0]
    q_parts = halves(q_rows[...])
    blank = jnp.zeros((128 - 2 * rank, model_dim), f32)
    none = jnp.zeros((rank, model_dim), f32)
    q_stacks = [
        jnp.concatenate(list(q_parts[: 2 - i]) + [none] * i + [blank], axis=0).astype(bf16)
        for i in range(2)
    ]
    left_turned = [jnp.zeros((ff, 128), f32)]

    def left_product(part):
        cols = slice(part * width, (part + 1) * width)
        for i, piece in enumerate(halves(merged[:, cols])):
            piece = piece.astype(bf16)
            splits[i, :, cols] = piece
            left_turned[0] += lax.dot_general(
                piece, q_stacks[i][:, cols], (((1,), (1,)), ((), ())), preferred_element_type=f32
            )

    for side in range(2):
        for step in range(nx):
            direct_copy(1, side, step, lax.rem(x + nx - step, nx)).wait_recv()
        for index, part in enumerate(kept[side]):
            merged[:, part * width : (part + 1) * width] += product(
                lhs_far[index], direct_in[1, side]
            )
            left_product(part)
    stacked = jnp.transpose(left_turned[0])
    left_local = stacked[rank : 2 * rank] + stacked[:rank]

    share = rank // replicas

    def dp_copy(source, target, stage, step, origin):
        return pltpu.make_async_remote_copy(
            src_ref=source,
            dst_ref=target.at[origin],
            send_sem=dp_send.at[stage, step - 1],
            recv_sem=dp_recv.at[stage, step - 1],
            device_id={"dp": lax.rem(replica + step, replicas)},
            device_id_type=MESH,
        )

    def begin_sum(value, out, into, stage):
        for row in range(rank):
            out[row // share, row % share] = value[row : row + 1]
        @pl.loop(1, replicas)
        def _(step):
            target = lax.rem(replica + step, replicas)
            dp_copy(out.at[target], into, stage, step, replica).start()

        into[replica] = out[replica]

    def end_sum(out, into, gathered, stage):
        @pl.loop(1, replicas)
        def _(step):
            origin = lax.rem(replica + replicas - step, replicas)
            dp_copy(out.at[0], into, stage, step, origin).wait_recv()

        total = into[0]
        for origin in range(1, replicas):
            total += into[origin]
        gathered[replica] = total * (1.0 / replicas)

        @pl.loop(1, replicas)
        def _(step):
            dp_copy(gathered.at[replica], gathered, stage + 1, step, replica).start()

    def collect(gathered, stage):
        @pl.loop(1, replicas)
        def _(step):
            origin = lax.rem(replica + replicas - step, replicas)
            dp_copy(gathered.at[replica], gathered, stage + 1, step, origin).wait_recv()

        return jnp.concatenate(
            [gathered[row // share, row % share] for row in range(rank)], axis=0
        )

    begin_sum(left_local, left_out, left_in, 0)
    save_merged = pltpu.make_async_copy(merged, merged_hbm, local_sem.at[3])
    save_merged.start()

    drain_x(half - 1, picked_near, arrived_near, range(2))
    for stage in range(2):
        for side in range(2):
            for step in range(nx):
                direct_copy(stage, side, step).wait_send()

    end_sum(left_out, left_in, left_all, 0)
    left_sum = collect(left_all, 0)

    left_parts = halves(left_sum)
    left_stack = jnp.concatenate(left_parts, axis=0).astype(bf16)
    right_local = None
    for i in (1, 0):
        terms = jnp.dot(left_stack[: (2 - i) * rank], splits[i], preferred_element_type=f32)
        for j in range(1 - i, -1, -1):
            term = terms[j * rank : (j + 1) * rank]
            right_local = term if right_local is None else right_local + term
    begin_sum(right_local, right_out, right_in, 2)

    gram = lax.dot_general(
        left_sum, left_sum, (((1,), (1,)), ((), ())),
        precision=highest, preferred_element_type=f32,
    )
    rows = lax.broadcasted_iota(jnp.int32, (rank, rank), 0)
    cols = lax.broadcasted_iota(jnp.int32, (rank, rank), 1)
    row_of = lax.broadcasted_iota(jnp.int32, (rank, 1), 0)
    inverse = jnp.where(rows == cols, 1.0, 0.0)
    pivots = jnp.zeros((rank, 1), f32)
    for k in range(rank):
        pivot = gram[k : k + 1, k : k + 1]
        pivots = jnp.where(row_of == k, pivot, pivots)
        ratio = jnp.where(row_of > k, gram[:, k : k + 1] / pivot, 0.0)
        gram, inverse = gram - ratio * gram[k : k + 1], inverse - ratio * inverse[k : k + 1]
    inverse = inverse / jnp.sqrt(pivots)
    i1, i2 = halves(inverse)
    inverse_stack = jnp.concatenate([i1, i1, i2], axis=1).astype(bf16)

    end_sum(right_out, right_in, right_all, 2)
    l1, l2 = left_parts
    basis = jnp.dot(
        inverse_stack, jnp.concatenate([l1, l2, l1], axis=0).astype(bf16),
        preferred_element_type=f32,
    )
    b1, b2 = halves(basis)
    blank = jnp.zeros((128 - 3 * rank, ff), f32)
    basis_stack[...] = jnp.transpose(
        jnp.concatenate([b1, b1, b2, blank], axis=0)
    ).astype(bf16)
    save_basis = pltpu.make_async_copy(basis_stack, basis_hbm, local_sem.at[4])
    save_basis.start()
    right_sum = collect(right_all, 2)
    r1, r2 = halves(right_sum)
    q_next[...] = jnp.dot(
        inverse_stack, jnp.concatenate([r1, r2, r1], axis=0).astype(bf16),
        preferred_element_type=f32,
    )
    save_merged.wait()
    save_basis.wait()
    for stage, source in enumerate((left_out, left_all, right_out, right_all)):
        @pl.loop(1, replicas)
        def _(step):
            dp_copy(source.at[0], source, stage, step, replica).wait_send()


def apply_kernel(
    merged_hbm, basis_hbm, q_hbm, error_hbm, next_hbm,
    merged, basis_stack, q_new, new_error, load_sem, small_sem, store_sem,
):
    rows = merged.shape[1]
    small = [
        pltpu.make_async_copy(q_hbm, q_new, small_sem.at[0]),
        pltpu.make_async_copy(basis_hbm, basis_stack, small_sem.at[1]),
    ]
    loads = [
        pltpu.make_async_copy(merged_hbm.at[pl.ds(i * rows, rows)], merged.at[i], load_sem.at[i])
        for i in range(STEPS)
    ]
    stores = [
        pltpu.make_async_copy(new_error.at[i], error_hbm.at[pl.ds(i * rows, rows)], store_sem.at[i])
        for i in range(STEPS)
    ]
    save_next = pltpu.make_async_copy(q_new, next_hbm, small_sem.at[2])
    for copy in small + loads:
        copy.start()
    small[0].wait()
    save_next.start()
    q1, q2 = halves(q_new[...])
    blank = jnp.zeros((128 - 3 * q1.shape[0], q1.shape[1]), f32)
    q_stack = jnp.concatenate([q1, q2, q1, blank], axis=0).astype(bf16)
    small[1].wait()
    for i in range(STEPS):
        loads[i].wait()
        approx = jnp.dot(
            basis_stack[i * rows : (i + 1) * rows], q_stack, preferred_element_type=f32
        )
        new_error[i] = (merged[i] - approx).astype(bf16)
        stores[i].start()
    save_next.wait()
    for copy in stores:
        copy.wait()


def shards(cotangent, route_weights, expert_ids, slot_index, hidden, carried_error, q_factor):
    peers = lax.axis_size("expert")
    replicas = lax.axis_size("dp")
    nx = X_CHIPS
    nz = peers // nx
    half = nz // 2
    tokens, model_dim = cotangent.shape[1:]
    capacity, ff = hidden.shape[2:]
    send = capacity // peers
    width = model_dim // PARTS
    vmem = pl.BlockSpec(memory_space=pltpu.VMEM)
    hbm = pl.BlockSpec(memory_space=pltpu.HBM)
    dma = pltpu.SemaphoreType.DMA
    rank = q_factor.shape[1]
    share = rank // replicas
    merged, basis_stack, q_new = pl.pallas_call(
        functools.partial(kernel, nz, nx, send, replicas),
        out_shape=(
            jax.ShapeDtypeStruct((ff, model_dim), f32),
            jax.ShapeDtypeStruct((ff, 128), bf16),
            jax.ShapeDtypeStruct((rank, model_dim), f32),
        ),
        in_specs=[hbm] * 7,
        out_specs=(hbm, hbm, vmem),
        scratch_shapes=[
            pltpu.VMEM(route_weights.shape[1:][::-1], f32),
            pltpu.VMEM(expert_ids.shape[1:][::-1], jnp.int32),
            pltpu.VMEM(slot_index.shape[1:][::-1], jnp.int32),
            pltpu.VMEM((rank, model_dim), f32),
            pltpu.VMEM((ff, 128), bf16),
            pltpu.VMEM((ff, model_dim), f32),
            pltpu.VMEM((2, ff, model_dim), bf16),
            pltpu.VMEM((tokens, model_dim), bf16),
            pltpu.VMEM((2, half - 1, PARTS, tokens, width), bf16),
            pltpu.VMEM((2, half, 16, 128), f32),
            pltpu.VMEM((32, 128), f32),
            pltpu.VMEM((half - 2, PARTS, nx, 2 * send, width), bf16),
            pltpu.VMEM((half - 2, PARTS, nx, 2 * send, width), bf16),
        ]
        + [pltpu.VMEM((PARTS, nx, PAD, width), bf16)] * 2
        + [pltpu.VMEM((2, nx, 2 * send, width), bf16)] * 2
        + [pltpu.VMEM((2, 2, nx, 2 * send, width), bf16)] * 2
        + [
            pltpu.VMEM((nz, nx * send, ff), bf16),
            pltpu.VMEM((ff, model_dim), bf16),
        ]
        + [pltpu.VMEM((replicas, share, 1, ff), f32)] * 3
        + [pltpu.VMEM((replicas, share, 1, model_dim), f32)] * 3
        + [
            dma((5,)),
            dma((4,)),
            dma((2, half - 1, PARTS)),
            dma((2, half - 1, PARTS)),
            dma((2, half - 1)),
            dma((2, half - 1)),
            dma((half, PARTS, nx - 1)),
            dma((half, PARTS, nx - 1)),
            dma((2, 2, nx)),
            dma((2, 2, nx)),
            dma((4, max(replicas - 1, 1))),
            dma((4, max(replicas - 1, 1))),
        ],
        compiler_params=pltpu.CompilerParams(
            collective_id=0, has_side_effects=True, vmem_limit_bytes=VMEM_BYTES
        ),
        name="route_and_factor",
    )(
        cotangent[0],
        route_weights[0].T,
        expert_ids[0].T,
        slot_index[0].T,
        hidden[0, 0].reshape(nz, nx * send, ff),
        carried_error[0, 0],
        q_factor[0],
    )
    rows = ff // STEPS
    new_error, q_next = pl.pallas_call(
        apply_kernel,
        out_shape=(
            jax.ShapeDtypeStruct((ff, model_dim), bf16),
            jax.ShapeDtypeStruct((rank, model_dim), f32),
        ),
        in_specs=[hbm] * 3,
        out_specs=(hbm, hbm),
        scratch_shapes=[
            pltpu.VMEM((STEPS, rows, model_dim), f32),
            pltpu.VMEM((ff, 128), bf16),
            pltpu.VMEM((rank, model_dim), f32),
            pltpu.VMEM((STEPS, rows, model_dim), bf16),
            dma((STEPS,)),
            dma((3,)),
            dma((STEPS,)),
        ],
        compiler_params=pltpu.CompilerParams(vmem_limit_bytes=VMEM_BYTES),
        name="apply_factors",
    )(merged, basis_stack, q_new)
    return (new_error[None, None], q_next[None])


def solution(mesh):
    return jax.shard_map(
        shards,
        mesh=mesh,
        in_specs=(
            P("dp", "expert", None),
            P("dp", "expert", None),
            P("dp", "expert", None),
            P("dp", "expert", None),
            P("dp", "expert", None, None),
            P("dp", "expert", None, None),
            P("expert", None, None),
        ),
        out_specs=(P("dp", "expert", None, None), P("expert", None, None)),
        check_vma=False,
    )
```

```python
import functools

import jax
import jax.numpy as jnp
from jax import lax
from jax.experimental import pallas as pl
from jax.experimental.pallas import tpu as pltpu
from jax.sharding import PartitionSpec as P

highest = lax.Precision.HIGHEST
MESH = pl.DeviceIdType.MESH
f32 = jnp.float32
bf16 = jnp.bfloat16

X_CHIPS = 4
PARTS = 4
VMEM_BYTES = 56 * 1024 * 1024
STEPS = 4
PAD = 32


def thirds(value):
    first = value.astype(bf16).astype(f32)
    second = (value - first).astype(bf16).astype(f32)
    return first, second, value - first - second


def halves(value):
    first = value.astype(bf16).astype(f32)
    return first, value - first


def kernel(
    nz, nx, send, replicas,
    cot, weights_hbm, ids_hbm, slots_hbm, hidden_hbm, error_hbm, q_hbm,
    merged_hbm, basis_hbm, q_next,
    weights, ids, slots, q_rows, basis_stack, merged, splits, own, ring, meta, own_meta, picked, arrived, picked_own, arrived_own, picked_near, arrived_near, direct_out, direct_in,
    hidden, error,
    left_out, left_in, left_all, right_out, right_in, right_all,
    local_sem, small_sem, ring_send, ring_recv, meta_send, meta_recv, x_send, x_recv,
    direct_send, direct_recv, dp_send, dp_recv,
):
    half = nz // 2
    tokens, model_dim = cot.shape
    width = model_dim // PARTS
    lanes = nx * send
    me = lax.axis_index("expert")
    z = lax.div(me, nx)
    x = lax.rem(me, nx)
    right = lax.rem(z + 1, nz) * nx + x
    left = lax.rem(z + nz - 1, nz) * nx + x
    sides = (right, left)

    load_hidden = pltpu.make_async_copy(hidden_hbm, hidden, local_sem.at[0])
    load_error = pltpu.make_async_copy(error_hbm, error, local_sem.at[1])
    load_own = pltpu.make_async_copy(cot, own, local_sem.at[2])
    load_own.start()
    load_small = [
        pltpu.make_async_copy(source, target, small_sem.at[i])
        for i, (source, target) in enumerate(
            ((ids_hbm, ids), (slots_hbm, slots), (weights_hbm, weights), (q_hbm, q_rows))
        )
    ]
    for load in load_small:
        load.start()

    barrier = pltpu.get_barrier_semaphore()
    levels = (lax.rem(z + 1, nz), lax.rem(z + nz - 1, nz))
    partners = [v * nx + lax.rem(x + step, nx) for step in range(nx) for v in levels]
    partners += [z * nx + lax.rem(x + step, nx) for step in range(1, nx)]
    for partner in partners:
        pl.semaphore_signal(barrier, inc=1, device_id={"expert": partner}, device_id_type=MESH)
    replica = lax.axis_index("dp")
    for step in sorted(range(1, replicas), key=lambda v: -min(v, replicas - v)):
        partner = lax.rem(replica + step, replicas)
        pl.semaphore_signal(barrier, inc=1, device_id={"dp": partner}, device_id_type=MESH)
    pl.semaphore_wait(barrier, len(partners) + replicas - 1)

    def ring_copy(side, hop, part, source=None):
        return pltpu.make_async_remote_copy(
            src_ref=ring.at[side, hop - 2, part] if source is None else source,
            dst_ref=ring.at[side, hop - 1, part],
            send_sem=ring_send.at[side, hop - 1, part],
            recv_sem=ring_recv.at[side, hop - 1, part],
            device_id={"expert": sides[side]},
            device_id_type=MESH,
        )

    def own_copy(side, part):
        return ring_copy(side, 1, part, own.at[:, pl.ds(part * width, width)])

    def meta_copy(side, hop):
        return pltpu.make_async_remote_copy(
            src_ref=meta.at[side, hop - 1],
            dst_ref=meta.at[side, hop],
            send_sem=meta_send.at[side, hop - 1],
            recv_sem=meta_recv.at[side, hop - 1],
            device_id={"expert": sides[side]},
            device_id_type=MESH,
        )

    def x_copy(pick, land, group, part, step, source=None):
        target = lax.rem(x + step, nx)
        source = x if source is None else source
        return pltpu.make_async_remote_copy(
            src_ref=pick.at[part, target],
            dst_ref=land.at[part, source],
            send_sem=x_send.at[group, part, step - 1],
            recv_sem=x_recv.at[group, part, step - 1],
            device_id={"expert": z * nx + target},
            device_id_type=MESH,
        )

    def direct_copy(stage, side, step, source=None):
        target = lax.rem(x + step, nx)
        source = x if source is None else source
        return pltpu.make_async_remote_copy(
            src_ref=direct_out.at[stage, side, target],
            dst_ref=direct_in.at[stage, side, source],
            send_sem=direct_send.at[stage, side, step],
            recv_sem=direct_recv.at[stage, side, step],
            device_id={"expert": levels[side] * nx + target},
            device_id_type=MESH,
        )

    load_own.wait()
    turn = PARTS // 2
    order = [(part, (part + turn) % PARTS) for part in range(PARTS)]
    kept = (range(turn), range(turn, PARTS))
    for parts in order:
        for side in range(2):
            own_copy(side, parts[side]).start()
    load_hidden.start()
    load_error.start()

    for load in load_small:
        load.wait()
    routes = ids.shape[0]
    spot = lax.broadcasted_iota(jnp.int32, (128, tokens), 0)
    token = lax.broadcasted_iota(jnp.int32, (128, tokens), 1).astype(f32)
    level = lax.div(ids[...], nx)
    place = lax.rem(ids[...], nx) * send + slots[...]
    to_right = lax.rem(level - z - 1 + 2 * nz, nz)
    to_left = lax.rem(z - level - 1 + 2 * nz, nz) + 16
    table = jnp.zeros((32, 512), f32)
    for k in range(routes):
        row = (spot[:32] == to_right[k : k + 1]) | (spot[:32] == to_left[k : k + 1])
        hit = spot == place[k : k + 1]
        values = [token] + [
            jnp.broadcast_to(v, (128, tokens)) for v in thirds(weights[k : k + 1, :])
        ]
        values = jnp.concatenate([jnp.where(hit, v, 0.0) for v in values], axis=0).astype(bf16)
        table += lax.dot_general(
            jnp.where(row, 1.0, 0.0).astype(bf16), values, (((1,), (1,)), ((), ())),
            preferred_element_type=f32,
        )
    which = table[:, :128]
    gain = (table[:, 384:] + table[:, 256:384]) + table[:, 128:256]
    for side in range(2):
        meta[side, 0, 0:8, :] = which[16 * side : 16 * side + 8]
        meta[side, 0, 8:16, :] = gain[16 * side : 16 * side + 8]
        meta_copy(side, 1).start()
    own_meta[0:16, :] = which[0:16]
    own_meta[16:32, :] = gain[0:16]

    token_lane = lax.broadcasted_iota(jnp.int32, (lanes, tokens), 1).astype(f32)

    def columns(rows):
        stacked = jnp.concatenate(rows + [jnp.zeros((8 - len(rows), 128), f32)], axis=0)
        turned = jnp.transpose(stacked)[:lanes]
        return [turned[:, i : i + 1] for i in range(len(rows))]

    def one_hot(which_column):
        return jnp.where(token_lane == which_column, 1.0, 0.0).astype(bf16)

    def pick_rows(blocks, pick, rows):
        chosen = [
            jnp.dot(choice, block, preferred_element_type=f32) * scale
            for choice, scale, block in blocks
        ]
        pad = rows - send * len(blocks)
        filler = [jnp.zeros((pad, width), f32)] if pad else []
        for target in range(nx):
            cut = [c[target * send : (target + 1) * send] for c in chosen]
            pick[target] = jnp.concatenate(cut + filler, axis=0).astype(bf16)

    def pass_rows(pick, land, group, part):
        for step in range(1, nx):
            x_copy(pick, land, group, part, step).start()
        land[part, x] = pick[part, x]

    def choices_of(hop, distance):
        got = columns(
            [meta[s, hop, pl.ds(distance - 1, 1), :] for s in range(2)]
            + [meta[s, hop, pl.ds(distance + 7, 1), :] for s in range(2)]
        )
        return [(one_hot(got[s]), got[2 + s]) for s in range(2)]

    def hidden_rows(levels, rows):
        blocks = [hidden[v].astype(f32) for v in levels]
        pad = rows - send * len(levels)
        filler = [jnp.zeros((pad, hidden.shape[2]), f32)] if pad else []
        pieces = []
        for source in range(nx):
            pieces += [b[source * send : (source + 1) * send] for b in blocks] + filler
        return jnp.transpose(jnp.concatenate(pieces, axis=0)).astype(bf16)

    def accumulate(land, pick, group, turned, rows, parts):
        for part in parts:
            for step in range(1, nx):
                x_copy(pick, land, group, part, step, lax.rem(x + nx - step, nx)).wait_recv()
            block = land[part].reshape(nx * rows, width)
            merged[:, pl.ds(part * width, width)] += jnp.dot(
                turned, block, preferred_element_type=f32
            )

    def pair_levels(hop):
        return [lax.rem(z - hop + nz, nz), lax.rem(z + hop, nz)]

    def step_hop(hop, forward, add):
        choices = None
        for slot, parts in enumerate(order):
            for side in range(2):
                ring_copy(side, hop, parts[side], own.at[:, pl.ds(0, width)]).wait_recv()
                if forward(side, parts[side]):
                    ring_copy(side, hop + 1, parts[side]).start()
            if choices is None:
                for side in range(2):
                    meta_copy(side, hop).wait_recv()
                    meta_copy(side, hop + 1).start()
                choices = choices_of(hop, hop)
            if slot < turn:
                add(parts)
            else:
                for part in parts:
                    blocks = [choices[s] + (ring[s, hop - 1, part],) for s in range(2)]
                    pick_rows(blocks, picked.at[hop - 1, part], 2 * send)
                    pass_rows(picked.at[hop - 1], arrived.at[hop - 1], hop - 1, part)

    def send_direct(stage, hop):
        choices = choices_of(hop, hop + 1)
        for side in range(2):
            parts = kept[side] if stage else kept[1 - side]
            blocks = [choices[side] + (ring[side, hop - 1, part],) for part in parts]
            pick_rows(blocks, direct_out.at[stage, side], 2 * send)
            for step in sorted(range(nx), key=lambda v: -min(v, nx - v)):
                direct_copy(stage, side, step).start()

    def adder(hop):
        turned = hidden_rows(pair_levels(hop), 2 * send)
        group = hop - 1

        def add(parts):
            accumulate(arrived.at[group], picked.at[group], group, turned, 2 * send, parts)

        return add

    everything = lambda side, part: True
    going_on = lambda side, part: part in kept[side]

    def drain_ring(hop, sent=everything):
        for part in range(PARTS):
            for side in range(2):
                if sent(side, part):
                    ring_copy(side, hop, part).wait_send()
        for side in range(2):
            meta_copy(side, hop).wait_send()

    def drain_x(group, pick, land, parts=range(PARTS)):
        for part in parts:
            for step in range(1, nx):
                x_copy(pick, land, group, part, step).wait_send()

    def drain_hop(hop):
        drain_x(hop - 1, picked.at[hop - 1], arrived.at[hop - 1])

    got = columns([own_meta[nz - 1 : nz, :], own_meta[nz + 15 : nz + 16, :]])
    own_choice = (one_hot(got[0]), got[1])
    for part in range(PARTS):
        block = own[:, part * width : (part + 1) * width]
        pick_rows([own_choice + (block,)], picked_own.at[part], PAD)
        pass_rows(picked_own, arrived_own, half - 2, part)
    load_error.wait()
    merged[...] = error[...].astype(f32)
    load_hidden.wait()

    turned_own = hidden_rows([z], PAD)
    add_own = lambda parts: accumulate(
        arrived_own, picked_own, half - 2, turned_own, PAD, parts
    )
    step_hop(1, everything, add_own)
    for part in range(PARTS):
        for side in range(2):
            own_copy(side, part).wait_send()
    for side in range(2):
        meta_copy(side, 1).wait_send()
    drain_x(half - 2, picked_own, arrived_own)

    def body(hop, carry):
        step_hop(hop, everything, adder(hop - 1))
        drain_ring(hop)
        drain_hop(hop - 1)
        return carry

    lax.fori_loop(2, half - 2, body, 0)
    step_hop(half - 2, going_on, adder(half - 3))
    send_direct(0, half - 2)
    drain_ring(half - 2)
    drain_hop(half - 3)

    for parts in order[:turn]:
        for side in range(2):
            ring_copy(side, half - 1, parts[side], own.at[:, pl.ds(0, width)]).wait_recv()
    for side in range(2):
        meta_copy(side, half - 1).wait_recv()
    send_direct(1, half - 1)
    choices = choices_of(half - 1, half - 1)
    for side in range(2):
        blocks = [choices[side] + (ring[side, half - 2, part],) for part in kept[side]]
        pick_rows(blocks, picked_near.at[side], 2 * send)
        pass_rows(picked_near, arrived_near, half - 1, side)
    adder(half - 2)(range(PARTS))
    drain_ring(half - 1, going_on)
    drain_hop(half - 2)

    def stacked_rows(level):
        block = hidden[level].astype(f32)
        pieces = [block[source * send : (source + 1) * send] for source in range(nx)]
        gap = jnp.zeros((send, hidden.shape[2]), f32)
        first = jnp.concatenate([p for piece in pieces for p in (piece, gap)], axis=0)
        second = jnp.concatenate([p for piece in pieces for p in (gap, piece)], axis=0)
        return [jnp.transpose(v).astype(bf16) for v in (first, second)]

    def product(lhs, buffer):
        rows = buffer.reshape(nx * 2 * send, width)
        return jnp.dot(lhs, rows, preferred_element_type=f32)

    before, after = pair_levels(half - 1)
    lhs_sides = [stacked_rows(before), stacked_rows(after)]
    lhs_far = stacked_rows(lax.rem(z + half, nz))
    for side in range(2):
        for step in range(1, nx):
            origin = lax.rem(x + nx - step, nx)
            x_copy(picked_near, arrived_near, half - 1, side, step, origin).wait_recv()
    for side in range(2):
        for step in range(nx):
            direct_copy(0, side, step, lax.rem(x + nx - step, nx)).wait_recv()
    for side in range(2):
        for index, part in enumerate(kept[side]):
            merged[:, part * width : (part + 1) * width] += product(
                lhs_sides[side][index], arrived_near[side]
            ) + product(lhs_sides[1 - side][index], direct_in[0, 1 - side])

    rank = q_rows.shape[0]
    ff = merged.shape[0]
    q_parts = halves(q_rows[...])
    blank = jnp.zeros((128 - 2 * rank, model_dim), f32)
    none = jnp.zeros((rank, model_dim), f32)
    q_stacks = [
        jnp.concatenate(list(q_parts[: 2 - i]) + [none] * i + [blank], axis=0).astype(bf16)
        for i in range(2)
    ]
    left_turned = [jnp.zeros((ff, 128), f32)]

    def left_product(part):
        cols = slice(part * width, (part + 1) * width)
        for i, piece in enumerate(halves(merged[:, cols])):
            piece = piece.astype(bf16)
            splits[i, :, cols] = piece
            left_turned[0] += lax.dot_general(
                piece, q_stacks[i][:, cols], (((1,), (1,)), ((), ())), preferred_element_type=f32
            )

    for side in range(2):
        for step in range(nx):
            direct_copy(1, side, step, lax.rem(x + nx - step, nx)).wait_recv()
        for index, part in enumerate(kept[side]):
            merged[:, part * width : (part + 1) * width] += product(
                lhs_far[index], direct_in[1, side]
            )
            left_product(part)
    stacked = jnp.transpose(left_turned[0])
    left_local = stacked[rank : 2 * rank] + stacked[:rank]

    share = rank // replicas

    def far_first(turn):
        return replicas // 2 + (2 * lax.rem(turn, 2) - 1) * lax.div(turn, 2)

    def dp_copy(source, target, stage, step, origin):
        return pltpu.make_async_remote_copy(
            src_ref=source,
            dst_ref=target.at[origin],
            send_sem=dp_send.at[stage, step - 1],
            recv_sem=dp_recv.at[stage, step - 1],
            device_id={"dp": lax.rem(replica + step, replicas)},
            device_id_type=MESH,
        )

    def begin_sum(value, out, into, stage):
        for row in range(rank):
            out[row // share, row % share] = value[row : row + 1]
        @pl.loop(1, replicas)
        def _(turn):
            step = far_first(turn)
            target = lax.rem(replica + step, replicas)
            dp_copy(out.at[target], into, stage, step, replica).start()

        into[replica] = out[replica]

    def end_sum(out, into, gathered, stage):
        @pl.loop(1, replicas)
        def _(step):
            origin = lax.rem(replica + replicas - step, replicas)
            dp_copy(out.at[0], into, stage, step, origin).wait_recv()

        total = into[0]
        for origin in range(1, replicas):
            total += into[origin]
        gathered[replica] = total * (1.0 / replicas)

        @pl.loop(1, replicas)
        def _(turn):
            dp_copy(gathered.at[replica], gathered, stage + 1, far_first(turn), replica).start()

    def collect(gathered, stage):
        @pl.loop(1, replicas)
        def _(step):
            origin = lax.rem(replica + replicas - step, replicas)
            dp_copy(gathered.at[replica], gathered, stage + 1, step, origin).wait_recv()

        return jnp.concatenate(
            [gathered[row // share, row % share] for row in range(rank)], axis=0
        )

    begin_sum(left_local, left_out, left_in, 0)
    save_merged = pltpu.make_async_copy(merged, merged_hbm, local_sem.at[3])
    save_merged.start()

    drain_x(half - 1, picked_near, arrived_near, range(2))
    for stage in range(2):
        for side in range(2):
            for step in range(nx):
                direct_copy(stage, side, step).wait_send()

    end_sum(left_out, left_in, left_all, 0)
    left_sum = collect(left_all, 0)

    left_parts = halves(left_sum)
    left_stack = jnp.concatenate(left_parts, axis=0).astype(bf16)
    right_local = None
    for i in (1, 0):
        terms = jnp.dot(left_stack[: (2 - i) * rank], splits[i], preferred_element_type=f32)
        for j in range(1 - i, -1, -1):
            term = terms[j * rank : (j + 1) * rank]
            right_local = term if right_local is None else right_local + term
    begin_sum(right_local, right_out, right_in, 2)

    gram = lax.dot_general(
        left_sum, left_sum, (((1,), (1,)), ((), ())),
        precision=highest, preferred_element_type=f32,
    )
    rows = lax.broadcasted_iota(jnp.int32, (rank, rank), 0)
    cols = lax.broadcasted_iota(jnp.int32, (rank, rank), 1)
    row_of = lax.broadcasted_iota(jnp.int32, (rank, 1), 0)
    inverse = jnp.where(rows == cols, 1.0, 0.0)
    pivots = jnp.zeros((rank, 1), f32)
    for k in range(rank):
        pivot = gram[k : k + 1, k : k + 1]
        pivots = jnp.where(row_of == k, pivot, pivots)
        ratio = jnp.where(row_of > k, gram[:, k : k + 1] / pivot, 0.0)
        gram, inverse = gram - ratio * gram[k : k + 1], inverse - ratio * inverse[k : k + 1]
    inverse = inverse / jnp.sqrt(pivots)
    i1, i2 = halves(inverse)
    inverse_stack = jnp.concatenate([i1, i1, i2], axis=1).astype(bf16)

    end_sum(right_out, right_in, right_all, 2)
    l1, l2 = left_parts
    basis = jnp.dot(
        inverse_stack, jnp.concatenate([l1, l2, l1], axis=0).astype(bf16),
        preferred_element_type=f32,
    )
    b1, b2 = halves(basis)
    blank = jnp.zeros((128 - 3 * rank, ff), f32)
    basis_stack[...] = jnp.transpose(
        jnp.concatenate([b1, b1, b2, blank], axis=0)
    ).astype(bf16)
    save_basis = pltpu.make_async_copy(basis_stack, basis_hbm, local_sem.at[4])
    save_basis.start()
    right_sum = collect(right_all, 2)
    r1, r2 = halves(right_sum)
    q_next[...] = jnp.dot(
        inverse_stack, jnp.concatenate([r1, r2, r1], axis=0).astype(bf16),
        preferred_element_type=f32,
    )
    save_merged.wait()
    save_basis.wait()
    for stage, source in enumerate((left_out, left_all, right_out, right_all)):
        @pl.loop(1, replicas)
        def _(step):
            dp_copy(source.at[0], source, stage, step, replica).wait_send()


def apply_kernel(
    merged_hbm, basis_hbm, q_hbm, error_hbm, next_hbm,
    merged, basis_stack, q_new, new_error, load_sem, small_sem, store_sem,
):
    rows = merged.shape[1]
    small = [
        pltpu.make_async_copy(q_hbm, q_new, small_sem.at[0]),
        pltpu.make_async_copy(basis_hbm, basis_stack, small_sem.at[1]),
    ]
    loads = [
        pltpu.make_async_copy(merged_hbm.at[pl.ds(i * rows, rows)], merged.at[i], load_sem.at[i])
        for i in range(STEPS)
    ]
    stores = [
        pltpu.make_async_copy(new_error.at[i], error_hbm.at[pl.ds(i * rows, rows)], store_sem.at[i])
        for i in range(STEPS)
    ]
    save_next = pltpu.make_async_copy(q_new, next_hbm, small_sem.at[2])
    for copy in small + loads:
        copy.start()
    small[0].wait()
    save_next.start()
    q1, q2 = halves(q_new[...])
    blank = jnp.zeros((128 - 3 * q1.shape[0], q1.shape[1]), f32)
    q_stack = jnp.concatenate([q1, q2, q1, blank], axis=0).astype(bf16)
    small[1].wait()
    for i in range(STEPS):
        loads[i].wait()
        approx = jnp.dot(
            basis_stack[i * rows : (i + 1) * rows], q_stack, preferred_element_type=f32
        )
        new_error[i] = (merged[i] - approx).astype(bf16)
        stores[i].start()
    save_next.wait()
    for copy in stores:
        copy.wait()


def shards(cotangent, route_weights, expert_ids, slot_index, hidden, carried_error, q_factor):
    peers = lax.axis_size("expert")
    replicas = lax.axis_size("dp")
    nx = X_CHIPS
    nz = peers // nx
    half = nz // 2
    tokens, model_dim = cotangent.shape[1:]
    capacity, ff = hidden.shape[2:]
    send = capacity // peers
    width = model_dim // PARTS
    vmem = pl.BlockSpec(memory_space=pltpu.VMEM)
    hbm = pl.BlockSpec(memory_space=pltpu.HBM)
    dma = pltpu.SemaphoreType.DMA
    rank = q_factor.shape[1]
    share = rank // replicas
    merged, basis_stack, q_new = pl.pallas_call(
        functools.partial(kernel, nz, nx, send, replicas),
        out_shape=(
            jax.ShapeDtypeStruct((ff, model_dim), f32),
            jax.ShapeDtypeStruct((ff, 128), bf16),
            jax.ShapeDtypeStruct((rank, model_dim), f32),
        ),
        in_specs=[hbm] * 7,
        out_specs=(hbm, hbm, vmem),
        scratch_shapes=[
            pltpu.VMEM(route_weights.shape[1:][::-1], f32),
            pltpu.VMEM(expert_ids.shape[1:][::-1], jnp.int32),
            pltpu.VMEM(slot_index.shape[1:][::-1], jnp.int32),
            pltpu.VMEM((rank, model_dim), f32),
            pltpu.VMEM((ff, 128), bf16),
            pltpu.VMEM((ff, model_dim), f32),
            pltpu.VMEM((2, ff, model_dim), bf16),
            pltpu.VMEM((tokens, model_dim), bf16),
            pltpu.VMEM((2, half - 1, PARTS, tokens, width), bf16),
            pltpu.VMEM((2, half, 16, 128), f32),
            pltpu.VMEM((32, 128), f32),
            pltpu.VMEM((half - 2, PARTS, nx, 2 * send, width), bf16),
            pltpu.VMEM((half - 2, PARTS, nx, 2 * send, width), bf16),
        ]
        + [pltpu.VMEM((PARTS, nx, PAD, width), bf16)] * 2
        + [pltpu.VMEM((2, nx, 2 * send, width), bf16)] * 2
        + [pltpu.VMEM((2, 2, nx, 2 * send, width), bf16)] * 2
        + [
            pltpu.VMEM((nz, nx * send, ff), bf16),
            pltpu.VMEM((ff, model_dim), bf16),
        ]
        + [pltpu.VMEM((replicas, share, 1, ff), f32)] * 3
        + [pltpu.VMEM((replicas, share, 1, model_dim), f32)] * 3
        + [
            dma((5,)),
            dma((4,)),
            dma((2, half - 1, PARTS)),
            dma((2, half - 1, PARTS)),
            dma((2, half - 1)),
            dma((2, half - 1)),
            dma((half, PARTS, nx - 1)),
            dma((half, PARTS, nx - 1)),
            dma((2, 2, nx)),
            dma((2, 2, nx)),
            dma((4, max(replicas - 1, 1))),
            dma((4, max(replicas - 1, 1))),
        ],
        compiler_params=pltpu.CompilerParams(
            collective_id=0, has_side_effects=True, vmem_limit_bytes=VMEM_BYTES
        ),
        name="route_and_factor",
    )(
        cotangent[0],
        route_weights[0].T,
        expert_ids[0].T,
        slot_index[0].T,
        hidden[0, 0].reshape(nz, nx * send, ff),
        carried_error[0, 0],
        q_factor[0],
    )
    rows = ff // STEPS
    new_error, q_next = pl.pallas_call(
        apply_kernel,
        out_shape=(
            jax.ShapeDtypeStruct((ff, model_dim), bf16),
            jax.ShapeDtypeStruct((rank, model_dim), f32),
        ),
        in_specs=[hbm] * 3,
        out_specs=(hbm, hbm),
        scratch_shapes=[
            pltpu.VMEM((STEPS, rows, model_dim), f32),
            pltpu.VMEM((ff, 128), bf16),
            pltpu.VMEM((rank, model_dim), f32),
            pltpu.VMEM((STEPS, rows, model_dim), bf16),
            dma((STEPS,)),
            dma((3,)),
            dma((STEPS,)),
        ],
        compiler_params=pltpu.CompilerParams(vmem_limit_bytes=VMEM_BYTES),
        name="apply_factors",
    )(merged, basis_stack, q_new)
    return (new_error[None, None], q_next[None])


def solution(mesh):
    return jax.shard_map(
        shards,
        mesh=mesh,
        in_specs=(
            P("dp", "expert", None),
            P("dp", "expert", None),
            P("dp", "expert", None),
            P("dp", "expert", None),
            P("dp", "expert", None, None),
            P("dp", "expert", None, None),
            P("expert", None, None),
        ),
        out_specs=(P("dp", "expert", None, None), P("expert", None, None)),
        check_vma=False,
    )
```
